512 devices in a mesh: tiles: 64 (over y, z), probe: 8 (over x, core).
Axes of the slice: x: 4, y: 4, z: 16, core: 2. Of those that a mesh axis runs over, the one named last changes fastest.
Arguments:
- coords: float32 [128, 2, 1024], P('tiles'), as said below
- noise_var: float32 [128, 1024], P('tiles'), may hold values from 0.25 to 1
- probes: float32 [128, 64, 1024], P('tiles', 'probe'), may hold values from -6 to 6
- pair_list: int32 [128, 4], P('tiles'), may hold values from -1 to 127, as said below
Outputs:
- solution: float32 [128, 64, 1024], P('tiles', 'probe')
- variance: float32 [128, 1024], P('tiles', 'probe')
The draws below stay inside these ranges and needn't reach their ends.
Inputs may be any that keep to these rules, and one draw needn't show every extreme that they name: `coords`: tile t lies in one unit cell of a grid 2 cells wide: the tiles t with t // 2 = g occupy 2 of the cells of grid rows 2 g and 2 g + 1, in raster order; its points lie inside its cell, the first coordinate being the column. pair_list[t, k] is the tile in the cell right of, below-left of, below, and below-right of tile t's cell for k = 0, 1, 2, 3, or -1 where that cell holds no tile.
All inputs are finite; a program needn't handle non-finite values.
Results may differ from the reference program's by a relative error of at most 0.0004.
Values may be sent and summed in bfloat16 or wider, within the bound.
A program may use at most 64 MiB of HBM per device.

```python
import math
import jax
import jax.numpy as jnp
from jax import lax

PTS = 1024
TILES_DEV = 2
PROBES = 64
ITERS = 2
TILES = 128
N_TILES = 64


def tile_cells(key):
    group_count = TILES // TILES_DEV
    group_keys = jax.random.split(key, group_count)

    def pick_cells(group_key):
        shuffled = jax.random.permutation(group_key, 2 * TILES_DEV)
        flags = (shuffled >= TILES_DEV).astype(jnp.int32)
        return jnp.argsort(flags, stable=True)[:TILES_DEV].astype(jnp.int32)
    chosen = jax.vmap(pick_cells)(group_keys)
    owners = jnp.arange(group_count, dtype=jnp.int32)[:, None]
    cell_rows = (2 * owners + chosen // TILES_DEV).reshape(-1)
    cell_cols = (chosen % TILES_DEV).reshape(-1)
    return (cell_rows, cell_cols)


def draw_coords(key, part):
    cell_rows, cell_cols = tile_cells(key)
    key = jax.random.fold_in(key, 7)
    offsets = jax.random.uniform(key, (TILES, 2, PTS), jnp.float32)
    corner = jnp.stack([cell_cols, cell_rows], axis=1).astype(jnp.float32)
    return corner[:, :, None] + offsets


def draw_pair_list(key, part):
    cell_rows, cell_cols = tile_cells(key)
    group_count = TILES // TILES_DEV
    cell_grid = jnp.full((2 * group_count + 1, TILES_DEV + 2), -1, jnp.int32)
    cell_grid = cell_grid.at[cell_rows, cell_cols + 1].set(jnp.arange(TILES, dtype=jnp.int32))
    right_cell = cell_grid[cell_rows, cell_cols + 2]
    below_left = cell_grid[cell_rows + 1, cell_cols]
    below_mid = cell_grid[cell_rows + 1, cell_cols + 1]
    below_right = cell_grid[cell_rows + 1, cell_cols + 2]
    return jnp.stack([right_cell, below_left, below_mid, below_right], axis=1)


def level_of(rng, extent, cuts, least, top_value):
    def one(dim, blocks):
        steps = jax.random.uniform(jax.random.fold_in(jax.random.fold_in(rng, 6), dim), (blocks,), jnp.float32, least / len(cuts), top_value / len(cuts))
        return jnp.repeat(jnp.exp(steps), extent[dim] // blocks).reshape((-1,) + (1,) * (len(extent) - dim - 1))

    level = one(*cuts[0])
    for cut in cuts[1:]:
        level = level * one(*cut)
    return level


def gaussian(key, dims, spread, reach, shards=(), kind=jnp.bfloat16):
    values = jax.random.normal(key, dims, jnp.float32) * spread
    if len(shards) > 0:
        values = level_of(key, dims, shards, -0.22, 0.18) * values
    return jnp.clip(values, min=-reach, max=reach).astype(kind)


def setup_inputs(seed: int = 0) -> dict:
    key_of = jax.random.split(jax.random.key(seed), 5)
    coords = draw_coords(jax.random.fold_in(key_of[4], 71), 0)
    noise_var = jnp.clip(jnp.exp(math.log(1.0) - 1.3862944 * jax.random.uniform(key_of[1], (TILES, PTS), jnp.float32) ** level_of(key_of[1], (TILES, PTS), ((0, 64),), -0.2, 0.2)), 0.25, 1.0)
    probes = gaussian(key_of[2], (TILES, PROBES, PTS), 1.0, 6.0, ((0, 64), (1, 8)), jnp.float32)
    pair_list = draw_pair_list(jax.random.fold_in(key_of[4], 71), 0)
    return dict(coords=coords, noise_var=noise_var, probes=probes, pair_list=pair_list)


support = 0.5

def kernel_weights(row_points, col_points):
    delta_x = row_points[:, 0, :, None] - col_points[:, 0, None, :]
    delta_y = row_points[:, 1, :, None] - col_points[:, 1, None, :]
    scaled = jnp.sqrt(delta_x * delta_x + delta_y * delta_y) / support
    return jnp.maximum(1.0 - scaled, 0.0) ** 4 * (4.0 * scaled + 1.0)

def reference(coords, noise_var, probes, pair_list):

    def operate(vector):
        vector_half = vector.astype(jnp.bfloat16)

        def group_terms(running, group_index):
            tiles_here = group_index * TILES_DEV + jnp.arange(TILES_DEV, dtype=jnp.int32)
            points_here = coords[tiles_here]
            self_block = kernel_weights(points_here, points_here).astype(jnp.bfloat16).astype(jnp.float32)
            self_terms = jnp.einsum('bij,bcj->bci', self_block, vector_half[tiles_here].astype(jnp.float32))
            partners = pair_list[tiles_here].reshape(-1)
            is_live = partners >= 0
            partner_idx = jnp.where(is_live, partners, 0).astype(jnp.int32)
            slot_tiles = jnp.repeat(tiles_here, 4).astype(jnp.int32)
            weights = kernel_weights(coords[slot_tiles], coords[partner_idx]) * is_live.astype(jnp.float32)[:, None, None]
            blocks = weights.astype(jnp.bfloat16).astype(jnp.float32)
            to_left = jnp.einsum('bij,bcj->bci', blocks, vector_half[partner_idx].astype(jnp.float32))
            to_right = jnp.einsum('bij,bci->bcj', blocks, vector_half[slot_tiles].astype(jnp.float32))
            running = running.at[tiles_here].add(self_terms)
            running = running.at[slot_tiles].add(to_left)
            running = running.at[partner_idx].add(to_right)
            return (running, group_index)
        kernel_terms = lax.scan(group_terms, jnp.zeros(vector.shape, jnp.float32), jnp.arange(N_TILES, dtype=jnp.int32))[0]
        return noise_var[:, None, :] * vector + kernel_terms

    def column_sums(left_part, right_part):
        return lax.optimization_barrier(jnp.sum(left_part * right_part, axis=(0, 2)))
    solution = jnp.zeros(probes.shape, jnp.float32)
    residual = probes
    direction = probes
    norm_now = column_sums(residual, residual)
    for sweep_index in range(ITERS):
        image_field = operate(direction)
        step_size = norm_now / column_sums(direction, image_field)
        solution = solution + step_size[None, :, None] * direction
        residual = residual - step_size[None, :, None] * image_field
        norm_next = column_sums(residual, residual)
        direction = residual + (norm_next / norm_now)[None, :, None] * direction
        norm_now = norm_next
    variance = lax.optimization_barrier(jnp.sum(probes * solution, axis=1)) / PROBES
    return (solution, variance)
```

```python
import functools
import jax
import jax.numpy as jnp
from jax import lax
from jax.experimental import pallas as pl
from jax.experimental.pallas import tpu as pltpu
from jax.sharding import PartitionSpec as P

F32 = jnp.float32
BF16 = jnp.bfloat16
MESH = pl.DeviceIdType.MESH

PTS = 1024
PROBES = 64
HALF = 8
CHIP = 16
NY, NZ, NX = 4, 16, 4
GROUPS = NY * NZ
LANES = 128
STRIPS = PTS // LANES

S_COORDS, S_Q, S_D, S_Z, S_ZX, S_AZ, S_AY, S_V = 0, 2, 7, 8, 11, 12, 27, 34
N_SEMS = 41


def fold(values):
    total = values[:, :LANES]
    for strip in range(1, STRIPS):
        total = total + values[:, strip * LANES : (strip + 1) * LANES]
    return total


def kernel(
    coords, noise, probes, pairs, sol, var,
    cbuf, lane, spread, nv, pv, qbuf, dbuf, qt, kbuf, zf, zb, zr, zx,
    az, ay, coef, vs, vr, lsem, ssem, rsem, s1, s2, s3,
):
    g = lax.axis_index("tiles")
    k = lax.axis_index("probe")
    y, z, x, c = g // NZ, lax.rem(g, NZ), k // 2, lax.rem(k, 2)
    other = 1 - c
    after, before = lax.rem(g + 1, GROUPS), lax.rem(g + GROUPS - 1, GROUPS)

    def at(dy=0, dz=0, dx=0, dc=0):
        return {
            "tiles": lax.rem(y + NY + dy, NY) * NZ + lax.rem(z + NZ + dz, NZ),
            "probe": lax.rem(x + NX + dx, NX) * 2 + lax.rem(c + dc, 2),
        }

    def signal(sem, device):
        pl.semaphore_signal(sem, inc=1, device_id=device, device_id_type=MESH)

    def copy(src, dst, index, device):
        return pltpu.make_async_remote_copy(
            src_ref=src, dst_ref=dst, send_sem=ssem.at[index], recv_sem=rsem.at[index],
            device_id=device, device_id_type=MESH,
        )

    loads = [
        pltpu.make_async_copy(src, dst, lsem.at[i])
        for i, (src, dst) in enumerate(((coords, cbuf.at[1]), (probes, pv), (noise, nv)))
    ]
    for load in loads:
        load.start()

    barrier = pltpu.get_barrier_semaphore()
    near = [
        {"tiles": after, "probe": k}, {"tiles": after, "probe": x * 2 + other},
        {"tiles": before, "probe": k}, {"tiles": before, "probe": x * 2 + other},
        at(dc=1), at(dz=1), at(dz=-1), at(dy=1), at(dy=-1), at(dx=1), at(dx=-1),
    ]
    for device in near:
        signal(barrier, device)

    def spread_rows(slot, tile):
        for axis in range(2):
            row = cbuf[1, tile, axis : axis + 1, :] * 8.0
            for b in range(STRIPS):
                cut = slice(b * LANES, (b + 1) * LANES)
                spread[slot, axis, cut, :] = jnp.broadcast_to(row[:, cut], (LANES, LANES)).T

    def fill(block, rows, cols):
        def step(r, carry):
            at_rows = pl.ds(pl.multiple_of(r * LANES, LANES), LANES)
            px, py = spread[rows, 0, at_rows, :], spread[rows, 1, at_rows, :]
            for b in range(STRIPS):
                cut = slice(b * LANES, (b + 1) * LANES)
                dx = px - lane[cols, 0:1, cut]
                dy = py - lane[cols, 1:2, cut]
                square = jnp.maximum(dx * dx + dy * dy, 1e-30)
                s4 = square * lax.rsqrt(square)
                m = jnp.maximum(4.0 - s4, 0.0)
                m = m * m
                kbuf[block, at_rows, cut] = ((m * m) * (s4 + 1.0)).astype(BF16)
            return carry

        lax.fori_loop(0, STRIPS, step, 0)

    def mul(field, block):
        return jnp.dot(field, kbuf[block], preferred_element_type=F32)

    def mul_t(field, block):
        return lax.dot_general(field, kbuf[block], (((1,), (1,)), ((), ())), preferred_element_type=F32)

    for load in loads:
        load.wait()
    qbuf[1, c] = pv[...].reshape(2 * HALF, PTS).astype(BF16)
    dbuf[c] = pv[c]
    lane[0] = cbuf[1, c] * 8.0
    spread_rows(0, c)
    fill(0, 0, 0)

    pl.semaphore_wait(barrier, len(near))
    sends = [
        copy(cbuf.at[1], cbuf.at[0], S_COORDS, near[0]),
        copy(cbuf.at[1], cbuf.at[2], S_COORDS + 1, near[2]),
        copy(qbuf.at[1, c], qbuf.at[1, c], S_Q, near[4]),
        copy(pv.at[other], dbuf.at[c], S_D, near[4]),
        copy(qbuf.at[1, c], qbuf.at[0, c], S_Q + 1, near[0]),
        copy(qbuf.at[1, c], qbuf.at[0, c], S_Q + 2, near[1]),
        copy(qbuf.at[1, c], qbuf.at[2, c], S_Q + 3, near[2]),
        copy(qbuf.at[1, c], qbuf.at[2, c], S_Q + 4, near[3]),
    ]
    for send in sends:
        send.start()
    for device in (at(dz=1), at(dz=-1), at(dy=-1), at(dx=-1), at(dc=1)):
        signal(s1, device)

    spread_rows(1, other)
    fill(1, 1, 0)

    def by_tile(group):
        first, second = qbuf[group, 0].astype(F32), qbuf[group, 1].astype(F32)
        return (
            jnp.concatenate([first[:HALF], second[:HALF]], 0),
            jnp.concatenate([first[HALF:], second[HALF:]], 0),
        )

    sends[2].wait_recv()
    t0, t1 = by_tile(1)
    qt[0] = jnp.where(c == 0, t0, t1).astype(BF16)
    qt[1] = jnp.where(c == 0, t1, t0).astype(BF16)
    zf[...] = mul(qt[0], 0) + mul(qt[1], 1)

    pl.semaphore_wait(s1, 5)
    for device in (at(dz=2), at(dz=-2), at(dc=1)):
        signal(s2, device)

    sends[0].wait_recv()
    sends[1].wait_recv()
    first_next = 2 * (g + 1)
    low = (pairs[c, 1] >= first_next) | (pairs[c, 2] >= first_next) | (pairs[c, 3] >= first_next)
    lane[1] = jnp.where(low, cbuf[2, c], cbuf[0, other]) * 8.0
    lane[2] = jnp.where(low, cbuf[2, other], cbuf[0, c]) * 8.0
    fill(2, 0, 1)

    pl.semaphore_wait(s2, 3)
    for device in (at(dz=4), at(dz=-4)):
        signal(s3, device)

    fill(3, 0, 2)
    for send in sends[4:]:
        send.wait_recv()
    p0, p1 = by_tile(0)
    n0, n1 = by_tile(2)
    qt[2] = jnp.where(low, jnp.where(c == 0, n0, n1), jnp.where(c == 0, p1, p0)).astype(BF16)
    qt[3] = jnp.where(low, jnp.where(c == 0, n1, n0), jnp.where(c == 0, p0, p1)).astype(BF16)
    sends[3].wait_recv()
    noise_row = nv[pl.ds(c, 1), :]
    start = dbuf[...].reshape(CHIP, PTS)
    image = noise_row * start + (zf[...] + mul_t(qt[2], 2) + mul_t(qt[3], 3)) * (1.0 / 256.0)
    zf[...] = image
    zb[...] = image.astype(BF16)

    fields = [
        copy(zb, zr.at[1], S_Z, near[2]),
        copy(zb, zr.at[2], S_Z + 1, near[1]),
        copy(zb, zr.at[0], S_Z + 2, near[4]),
        copy(zf.at[pl.ds(pl.multiple_of(other * HALF, HALF), HALF), :], zx, S_ZX, near[4]),
    ]
    for send in fields:
        send.start()
    second = mul(zb[...], 0)
    pl.semaphore_wait(s3, 2)
    fields[2].wait_recv()
    second = second + mul(zr[0], 1)
    fields[0].wait_recv()
    fields[1].wait_recv()
    across = jnp.where(low, zr[1].astype(F32), zr[2].astype(F32)).astype(BF16)
    second = second + 2.0 * mul_t(across, 2)
    second = second * (1.0 / 256.0) + noise_row * image

    moments = jnp.concatenate(
        [fold(start * start), fold(start * image), fold(image * image), fold(image * second), jnp.zeros((64, LANES), F32)], 0
    )
    az[0] = jnp.sum(moments.T, axis=0, keepdims=True)
    along_z = [copy(az.at[0], az.at[d], S_AZ + d - 1, at(dz=d)) for d in range(1, NZ)]
    for d in (8, 7, 9, 6, 10, 5, 11, 4, 12, 3, 13, 2, 14, 1, 15):
        along_z[d - 1].start()
    for send in along_z:
        send.wait_recv()
    ay[0] = jnp.sum(az[...], axis=0)
    steps = [(dy, dc) for dy in range(NY) for dc in range(2)][1:]
    along_y = [copy(ay.at[0], ay.at[j + 1], S_AY + j, at(dy=dy, dc=dc)) for j, (dy, dc) in enumerate(steps)]
    for j in (3, 4, 1, 2, 5, 6, 0):
        along_y[j].start()
    for send in along_y:
        send.wait_recv()
    m0 = jnp.sum(ay[...], axis=0)
    m1, m2, m3 = (pltpu.roll(m0, LANES - CHIP * i, 1) for i in (1, 2, 3))
    step0 = m0 / m1
    growth = m2 / m1
    step1 = (m2 - m1 * m1 / m0) / (m3 - m2 * growth)
    for i, value in enumerate((step0 + step0 * step1 * growth, -step0 * step1)):
        coef[i] = jnp.broadcast_to(value, (LANES, LANES)).T

    mine = pl.ds(pl.multiple_of(c * HALF, HALF), HALF)
    alpha = jnp.concatenate([coef[0, mine, :]] * STRIPS, 1)
    beta = jnp.concatenate([coef[1, mine, :]] * STRIPS, 1)
    fields[3].wait_recv()
    for tile, held in ((c, zf[mine, :]), (other, zx[...])):
        begin = pv[tile]
        result = alpha * begin + beta * held
        sol[tile] = result
        total = jnp.sum(begin * result, axis=0, keepdims=True) * (1.0 / PROBES)
        for j in range(STRIPS):
            vs[j, pl.ds(tile, 1), :] = total[:, j * LANES : (j + 1) * LANES]
    across_x = []
    for j, (dx, dc) in enumerate([(dx, dc) for dx in range(NX) for dc in range(2)][1:]):
        device = at(dx=dx, dc=dc)
        across_x.append(copy(vs.at[device["probe"]], vr.at[j], S_V + j, device))
    for send in across_x:
        send.start()
    for send in across_x:
        send.wait_recv()
    var[...] = vs[k] + jnp.sum(vr[...], axis=0)
    for send in sends + fields + along_z + along_y + across_x:
        send.wait_send()


def shards(coords, noise_var, probes, pair_list):
    anywhere = pl.BlockSpec(memory_space=pl.ANY)
    return pl.pallas_call(
        kernel,
        out_shape=(
            jax.ShapeDtypeStruct(probes.shape, F32),
            jax.ShapeDtypeStruct((2, LANES), F32),
        ),
        in_specs=[anywhere, anywhere, anywhere, pl.BlockSpec(memory_space=pltpu.SMEM)],
        out_specs=[pl.BlockSpec(memory_space=pltpu.VMEM)] * 2,
        scratch_shapes=[
            pltpu.VMEM((3, 2, 2, PTS), F32),
            pltpu.VMEM((3, 2, PTS), F32),
            pltpu.VMEM((2, 2, PTS, LANES), F32),
            pltpu.VMEM((2, PTS), F32),
            pltpu.VMEM((2, HALF, PTS), F32),
            pltpu.VMEM((3, 2, 2 * HALF, PTS), BF16),
            pltpu.VMEM((2, HALF, PTS), F32),
            pltpu.VMEM((4, CHIP, PTS), BF16),
            pltpu.VMEM((4, PTS, PTS), BF16),
            pltpu.VMEM((CHIP, PTS), F32),
            pltpu.VMEM((CHIP, PTS), BF16),
            pltpu.VMEM((3, CHIP, PTS), BF16),
            pltpu.VMEM((HALF, PTS), F32),
            pltpu.VMEM((NZ, 1, LANES), F32),
            pltpu.VMEM((8, 1, LANES), F32),
            pltpu.VMEM((2, LANES, LANES), F32),
            pltpu.VMEM((8, 2, LANES), F32),
            pltpu.VMEM((7, 2, LANES), F32),
            pltpu.SemaphoreType.DMA((3,)),
            pltpu.SemaphoreType.DMA((N_SEMS,)),
            pltpu.SemaphoreType.DMA((N_SEMS,)),
            pltpu.SemaphoreType.REGULAR,
            pltpu.SemaphoreType.REGULAR,
            pltpu.SemaphoreType.REGULAR,
        ],
        compiler_params=pltpu.CompilerParams(
            collective_id=0, has_side_effects=True, vmem_limit_bytes=32 << 20
        ),
    )(coords, noise_var, probes, pair_list)


def solution(mesh):
    in_specs = (
        P("tiles", None, None),
        P("tiles", None),
        P("tiles", "probe", None),
        P("tiles", None),
    )
    out_specs = (P("tiles", "probe", None), P("tiles", "probe"))
    return jax.shard_map(shards, mesh=mesh, in_specs=in_specs, out_specs=out_specs, check_vma=False)
```

```python
import functools
import jax
import jax.numpy as jnp
from jax import lax
from jax.experimental import pallas as pl
from jax.experimental.pallas import tpu as pltpu
from jax.sharding import PartitionSpec as P

F32 = jnp.float32
BF16 = jnp.bfloat16
MESH = pl.DeviceIdType.MESH

PTS = 1024
PROBES = 64
HALF = 8
CHIP = 16
NY, NZ, NX = 4, 16, 4
GROUPS = NY * NZ
LANES = 128
STRIPS = PTS // LANES

S_COORDS, S_Q, S_D, S_Z, S_ZX, S_P, S_AZ, S_AY = 0, 2, 7, 8, 11, 12, 19, 50
N_SEMS = 65


def fold(values):
    total = values[:, :LANES]
    for strip in range(1, STRIPS):
        total = total + values[:, strip * LANES : (strip + 1) * LANES]
    return total


def kernel(
    coords, noise, probes, pairs, sol, var,
    cbuf, lane, spread, nv, pv, qbuf, dbuf, qt, k_self, k_pair, k_near, k_far, zf, zb, zr, zx,
    az, ay, coef, ps, pr, lsem, ssem, rsem, s1, s2, s3,
):
    g = lax.axis_index("tiles")
    k = lax.axis_index("probe")
    y, z, x, c = g // NZ, lax.rem(g, NZ), k // 2, lax.rem(k, 2)
    other = 1 - c
    after, before = lax.rem(g + 1, GROUPS), lax.rem(g + GROUPS - 1, GROUPS)

    def at(dy=0, dz=0, dx=0, dc=0):
        return {
            "tiles": lax.rem(y + NY + dy, NY) * NZ + lax.rem(z + NZ + dz, NZ),
            "probe": lax.rem(x + NX + dx, NX) * 2 + lax.rem(c + dc, 2),
        }

    def signal(sem, device):
        pl.semaphore_signal(sem, inc=1, device_id=device, device_id_type=MESH)

    def copy(src, dst, index, device):
        return pltpu.make_async_remote_copy(
            src_ref=src, dst_ref=dst, send_sem=ssem.at[index], recv_sem=rsem.at[index],
            device_id=device, device_id_type=MESH,
        )

    loads = [
        pltpu.make_async_copy(src, dst, lsem.at[i])
        for i, (src, dst) in enumerate(((coords, cbuf.at[1]), (probes, pv), (noise, nv)))
    ]
    for load in loads:
        load.start()

    barrier = pltpu.get_barrier_semaphore()
    near = [
        {"tiles": after, "probe": k}, {"tiles": after, "probe": x * 2 + other},
        {"tiles": before, "probe": k}, {"tiles": before, "probe": x * 2 + other},
        at(dc=1), at(dz=1), at(dz=-1), at(dz=1, dc=1), at(dz=-1, dc=1),
        at(dy=1), at(dy=-1), at(dx=1), at(dx=-1),
    ]
    for device in near:
        signal(barrier, device)

    def fill(block, cols, low=0, high=STRIPS):
        def step(r, carry):
            at_rows = pl.ds(pl.multiple_of(r * LANES, LANES), LANES)
            px, py = spread[0, at_rows, :], spread[1, at_rows, :]
            for b in range(STRIPS):
                cut = slice(b * LANES, (b + 1) * LANES)
                dx = px - lane[cols, 0:1, cut]
                dy = py - lane[cols, 1:2, cut]
                square = jnp.maximum(dx * dx + dy * dy, 1e-30)
                s4 = square * lax.rsqrt(square)
                m = jnp.maximum(4.0 - s4, 0.0)
                m = m * m
                block[at_rows, cut] = ((m * m) * (s4 + 1.0)).astype(BF16)
            return carry

        lax.fori_loop(low, high, step, 0)

    def times_rows(field, block):
        return lax.dot_general(
            field[...], block[...], (((1,), (1,)), ((), ())), preferred_element_type=F32
        )

    def times(field, block):
        return jnp.dot(field[...], block[...], preferred_element_type=F32)

    for load in loads:
        load.wait()
    lane[0] = cbuf[1, c] * 8.0
    for axis in range(2):
        for b in range(STRIPS):
            cut = slice(b * LANES, (b + 1) * LANES)
            spread[axis, cut, :] = jnp.broadcast_to(lane[0, axis : axis + 1, cut], (LANES, LANES)).T
    qbuf[1, c] = pv[...].reshape(2 * HALF, PTS).astype(BF16)
    dbuf[c] = pv[c]
    lane[1] = cbuf[1, other] * 8.0
    fill(k_self, 0, 0, 3)

    pl.semaphore_wait(barrier, len(near))
    sends = [
        copy(cbuf.at[1], cbuf.at[0], S_COORDS, near[0]),
        copy(cbuf.at[1], cbuf.at[2], S_COORDS + 1, near[2]),
        copy(qbuf.at[1, c], qbuf.at[1, c], S_Q, near[4]),
        copy(pv.at[other], dbuf.at[c], S_D, near[4]),
        copy(qbuf.at[1, c], qbuf.at[0, c], S_Q + 1, near[0]),
        copy(qbuf.at[1, c], qbuf.at[0, c], S_Q + 2, near[1]),
        copy(qbuf.at[1, c], qbuf.at[2, c], S_Q + 3, near[2]),
        copy(qbuf.at[1, c], qbuf.at[2, c], S_Q + 4, near[3]),
    ]
    for send in sends:
        send.start()
    for device in (at(dz=1), at(dz=-1), at(dy=-1), at(dx=-1), at(dx=1)):
        signal(s1, device)

    fill(k_self, 0, 3)
    fill(k_pair, 1)

    def by_tile(group):
        first, second = qbuf[group, 0].astype(F32), qbuf[group, 1].astype(F32)
        return (
            jnp.concatenate([first[:HALF], second[:HALF]], 0),
            jnp.concatenate([first[HALF:], second[HALF:]], 0),
        )

    pl.semaphore_wait(s1, 5)
    for device in (at(dz=2), at(dz=-2), at(dx=-1), at(dx=1)):
        signal(s2, device)
    sends[2].wait_recv()
    t0, t1 = by_tile(1)
    qt[0] = jnp.where(c == 0, t0, t1).astype(BF16)
    qt[1] = jnp.where(c == 0, t1, t0).astype(BF16)
    zf[...] = times(qt.at[0], k_self) + times_rows(qt.at[1], k_pair)

    sends[0].wait_recv()
    sends[1].wait_recv()
    first_next = 2 * (g + 1)
    low = (pairs[c, 1] >= first_next) | (pairs[c, 2] >= first_next) | (pairs[c, 3] >= first_next)
    lane[2] = jnp.where(low, cbuf[2, c], cbuf[0, other]) * 8.0
    lane[3] = jnp.where(low, cbuf[2, other], cbuf[0, c]) * 8.0
    fill(k_near, 2)

    pl.semaphore_wait(s2, 4)
    for device in (at(dz=4), at(dz=-4), at(dx=-1)):
        signal(s3, device)
    fill(k_far, 3)
    for send in sends[4:]:
        send.wait_recv()
    p0, p1 = by_tile(0)
    n0, n1 = by_tile(2)
    qt[2] = jnp.where(low, jnp.where(c == 0, n0, n1), jnp.where(c == 0, p1, p0)).astype(BF16)
    qt[3] = jnp.where(low, jnp.where(c == 0, n1, n0), jnp.where(c == 0, p0, p1)).astype(BF16)
    sends[3].wait_recv()
    noise_row = nv[pl.ds(c, 1), :]
    start = dbuf[...].reshape(CHIP, PTS)
    image = zf[...] + times_rows(qt.at[2], k_near) + times_rows(qt.at[3], k_far)
    image = noise_row * start + image * (1.0 / 256.0)
    zf[...] = image
    zb[...] = image.astype(BF16)

    fields = [
        copy(zb, zr.at[1], S_Z, near[2]),
        copy(zb, zr.at[2], S_Z + 1, near[1]),
        copy(zb, zr.at[0], S_Z + 2, near[4]),
        copy(zf.at[pl.ds(pl.multiple_of(other * HALF, HALF), HALF), :], zx, S_ZX, near[4]),
    ]
    for send in fields:
        send.start()
    products = (start * start, start * image)
    for j in range(STRIPS):
        for i in range(2):
            ps[j, i] = products[i][:, j * LANES : (j + 1) * LANES]
    shares = []
    for j, (dx, dc) in enumerate([(dx, dc) for dx in range(NX) for dc in range(2)][1:]):
        device = at(dx=dx, dc=dc)
        shares.append(copy(ps.at[device["probe"]], pr.at[j], S_P + j, device))
    for send in shares:
        send.start()

    moments = [fold(products[0]), fold(products[1]), fold(image * image)]
    square = fold(image * (times(zb, k_self) * (1.0 / 256.0) + noise_row * image))
    to_pair, to_near = times(zb, k_pair), times(zb, k_near)
    pl.semaphore_wait(s3, 3)
    fields[2].wait_recv()
    square = square + fold(to_pair * zr[0].astype(F32)) * (1.0 / 256.0)
    fields[0].wait_recv()
    fields[1].wait_recv()
    across = jnp.where(low, zr[1].astype(F32), zr[2].astype(F32))
    square = square + fold(to_near * across) * (2.0 / 256.0)

    table = jnp.concatenate(moments + [square, jnp.zeros((64, LANES), F32)], 0)
    az[0] = jnp.sum(table.T, axis=0, keepdims=True)
    along_z = [copy(az.at[0], az.at[i], S_AZ + i - 1, at(dz=i // 2, dc=i % 2)) for i in range(1, 2 * NZ)]
    for i in sorted(range(1, 2 * NZ), key=lambda i: -min(i // 2, NZ - i // 2)):
        along_z[i - 1].start()
    for send in along_z:
        send.wait_recv()
    ay[0] = jnp.sum(az[...], axis=0)
    plane = [copy(ay.at[0], ay.at[i], S_AY + i - 1, at(dx=i // NY, dy=i % NY)) for i in range(1, NX * NY)]
    for i in sorted(range(1, NX * NY), key=lambda i: -(min(i // NY, NX - i // NY) + min(i % NY, NY - i % NY))):
        plane[i - 1].start()
    for send in plane:
        send.wait_recv()
    m0 = jnp.concatenate([jnp.sum(ay[NY * i : NY * (i + 1)], axis=0) for i in range(NX)], 0)
    m1, m2, m3 = (pltpu.roll(m0, LANES - CHIP * i, 1) for i in (1, 2, 3))
    step0 = m0 / m1
    growth = m2 / m1
    step1 = (m2 - m1 * m1 / m0) / (m3 - m2 * growth)
    alpha, beta = step0 + step0 * step1 * growth, -step0 * step1
    at_lane = lax.broadcasted_iota(jnp.int32, (1, LANES), 1)
    packed = jnp.zeros((1, LANES), F32)
    for i in range(NX):
        for h, value in enumerate((alpha, beta)):
            first = 32 * i + CHIP * h
            row = value[i : i + 1]
            if first:
                row = pltpu.roll(row, first, 1)
            packed = jnp.where((at_lane >= first) & (at_lane < first + CHIP), row, packed)
    coef[...] = jnp.broadcast_to(packed, (LANES, LANES)).T

    mine = pl.ds(pl.multiple_of(c * HALF, HALF), HALF)
    alpha_mine = jnp.concatenate([coef[mine, :]] * STRIPS, 1)
    beta_mine = jnp.concatenate([coef[pl.ds(pl.multiple_of(CHIP + c * HALF, HALF), HALF), :]] * STRIPS, 1)
    fields[3].wait_recv()
    sol[c] = alpha_mine * pv[c] + beta_mine * zf[mine, :]
    sol[other] = alpha_mine * pv[other] + beta_mine * zx[...]
    for send in shares:
        send.wait_recv()
    for dc, tile in ((0, c), (1, other)):
        total = jnp.zeros((CHIP, LANES), F32)
        for dx in range(NX):
            share = ps.at[k] if (dx, dc) == (0, 0) else pr.at[2 * dx + dc - 1]
            total = total + coef[32 * dx : 32 * dx + CHIP, :] * share[0]
            total = total + coef[32 * dx + CHIP : 32 * dx + 2 * CHIP, :] * share[1]
        var[pl.ds(tile, 1), :] = jnp.sum(total, axis=0, keepdims=True) * (1.0 / PROBES)
    for send in sends + fields + shares + along_z + plane:
        send.wait_send()


def shards(coords, noise_var, probes, pair_list):
    anywhere = pl.BlockSpec(memory_space=pl.ANY)
    return pl.pallas_call(
        kernel,
        out_shape=(
            jax.ShapeDtypeStruct(probes.shape, F32),
            jax.ShapeDtypeStruct((2, LANES), F32),
        ),
        in_specs=[anywhere, anywhere, anywhere, pl.BlockSpec(memory_space=pltpu.SMEM)],
        out_specs=[pl.BlockSpec(memory_space=pltpu.VMEM)] * 2,
        scratch_shapes=[
            pltpu.VMEM((3, 2, 2, PTS), F32),
            pltpu.VMEM((4, 2, PTS), F32),
            pltpu.VMEM((2, PTS, LANES), F32),
            pltpu.VMEM((2, PTS), F32),
            pltpu.VMEM((2, HALF, PTS), F32),
            pltpu.VMEM((3, 2, 2 * HALF, PTS), BF16),
            pltpu.VMEM((2, HALF, PTS), F32),
            pltpu.VMEM((4, CHIP, PTS), BF16),
            pltpu.VMEM((PTS, PTS), BF16),
            pltpu.VMEM((PTS, PTS), BF16),
            pltpu.VMEM((PTS, PTS), BF16),
            pltpu.VMEM((PTS, PTS), BF16),
            pltpu.VMEM((CHIP, PTS), F32),
            pltpu.VMEM((CHIP, PTS), BF16),
            pltpu.VMEM((3, CHIP, PTS), BF16),
            pltpu.VMEM((HALF, PTS), F32),
            pltpu.VMEM((2 * NZ, 1, LANES), F32),
            pltpu.VMEM((NX * NY, 1, LANES), F32),
            pltpu.VMEM((LANES, LANES), F32),
            pltpu.VMEM((8, 2, CHIP, LANES), F32),
            pltpu.VMEM((7, 2, CHIP, LANES), F32),
            pltpu.SemaphoreType.DMA((3,)),
            pltpu.SemaphoreType.DMA((N_SEMS,)),
            pltpu.SemaphoreType.DMA((N_SEMS,)),
            pltpu.SemaphoreType.REGULAR,
            pltpu.SemaphoreType.REGULAR,
            pltpu.SemaphoreType.REGULAR,
        ],
        compiler_params=pltpu.CompilerParams(
            collective_id=0, has_side_effects=True, vmem_limit_bytes=32 << 20
        ),
    )(*(pltpu.with_memory_space_constraint(v, pltpu.MemorySpace.HBM) for v in (coords, noise_var, probes, pair_list)))


def solution(mesh):
    in_specs = (
        P("tiles", None, None),
        P("tiles", None),
        P("tiles", "probe", None),
        P("tiles", None),
    )
    out_specs = (P("tiles", "probe", None), P("tiles", "probe"))
    return jax.shard_map(shards, mesh=mesh, in_specs=in_specs, out_specs=out_specs, check_vma=False)
```

```python
import functools
import jax
import jax.numpy as jnp
from jax import lax
from jax.experimental import pallas as pl
from jax.experimental.pallas import tpu as pltpu
from jax.sharding import PartitionSpec as P

F32 = jnp.float32
BF16 = jnp.bfloat16
MESH = pl.DeviceIdType.MESH

PTS = 1024
PROBES = 64
HALF = 8
CHIP = 16
NY, NZ, NX = 4, 16, 4
GROUPS = NY * NZ
LANES = 128
STRIPS = PTS // LANES
MID = PTS // 2
HALVES = (slice(0, MID), slice(MID, PTS))

S_COORDS, S_Q, S_D, S_Z, S_ZX, S_P, S_AZ, S_AY, S_T = 0, 2, 7, 8, 11, 12, 13, 14, 15
N_SEMS = 16


def fold(values):
    total = values[:, :LANES]
    for strip in range(1, STRIPS):
        total = total + values[:, strip * LANES : (strip + 1) * LANES]
    return total


def kernel(
    coords, noise, probes, pair_list, sol, var,
    pairs, cbuf, lane, spread, nv, pv, qbuf, dbuf, qt, k_self, k_pair, k_near, k_far, zf, zp, zo, zb, zr, zx,
    az, ay, coef, ps, pr, lsem, ssem, rsem, s1, s2, s3,
):
    g = lax.axis_index("tiles")
    k = lax.axis_index("probe")
    y, z, x, c = g // NZ, lax.rem(g, NZ), k // 2, lax.rem(k, 2)
    other = 1 - c
    after, before = lax.rem(g + 1, GROUPS), lax.rem(g + GROUPS - 1, GROUPS)

    def at(dy=0, dz=0, dx=0, dc=0):
        return {
            "tiles": lax.rem(y + NY + dy, NY) * NZ + lax.rem(z + NZ + dz, NZ),
            "probe": lax.rem(x + NX + dx, NX) * 2 + lax.rem(c + dc, 2),
        }

    def signal(sem, device):
        pl.semaphore_signal(sem, inc=1, device_id=device, device_id_type=MESH)

    def copy(src, dst, index, device):
        return pltpu.make_async_remote_copy(
            src_ref=src, dst_ref=dst, send_sem=ssem.at[index], recv_sem=rsem.at[index],
            device_id=device, device_id_type=MESH,
        )

    loads = [
        pltpu.make_async_copy(src, dst, lsem.at[i])
        for i, (src, dst) in enumerate(((coords, cbuf.at[1]), (probes, pv), (noise, nv), (pair_list, pairs)))
    ]
    for load in loads:
        load.start()

    barrier = pltpu.get_barrier_semaphore()
    near = [
        {"tiles": after, "probe": k}, {"tiles": after, "probe": x * 2 + other},
        {"tiles": before, "probe": k}, {"tiles": before, "probe": x * 2 + other},
        at(dc=1), at(dz=1), at(dz=-1), at(dz=1, dc=1), at(dz=-1, dc=1),
        at(dy=1), at(dy=-1), at(dx=1), at(dx=-1),
    ]
    for device in near:
        signal(barrier, device)

    def in_order(values):
        return jnp.where(c == 0, values, jnp.concatenate([values[:, MID:], values[:, :MID]], 1))

    def fill(block, cols, low=0, high=STRIPS, strips=range(STRIPS)):
        def step(r, carry):
            at_rows = pl.ds(pl.multiple_of(r * LANES, LANES), LANES)
            px, py = spread[0, at_rows, :], spread[1, at_rows, :]
            for b in strips:
                cut = slice(b * LANES, (b + 1) * LANES)
                dx = px - lane[cols, 0:1, cut]
                dy = py - lane[cols, 1:2, cut]
                square = jnp.maximum(dx * dx + dy * dy, 1e-30)
                s4 = square * lax.rsqrt(square)
                m = jnp.maximum(4.0 - s4, 0.0)
                m = m * m
                block[at_rows, cut] = ((m * m) * (s4 + 1.0)).astype(BF16)
            return carry

        lax.fori_loop(low, high, step, 0)

    def times_rows(field, block):
        return lax.dot_general(
            field[...], block[...], (((1,), (1,)), ((), ())), preferred_element_type=F32
        )

    def times(field, block):
        return jnp.dot(field[...], block[...], preferred_element_type=F32)

    loads[0].wait()
    loads[1].wait()
    lane[0] = cbuf[1, c] * 8.0
    for axis in range(2):
        for b in range(STRIPS):
            cut = slice(b * LANES, (b + 1) * LANES)
            spread[axis, cut, :] = jnp.broadcast_to(lane[0, axis : axis + 1, cut], (LANES, LANES)).T
    qbuf[1, c] = pv[...].reshape(2 * HALF, PTS).astype(BF16)
    dbuf[c] = pv[c]
    lane[1] = in_order(cbuf[1, other]) * 8.0
    fill(k_self, 0, 0, 3)

    pl.semaphore_wait(barrier, len(near))
    sends = [
        copy(cbuf.at[1], cbuf.at[0], S_COORDS, near[0]),
        copy(cbuf.at[1], cbuf.at[2], S_COORDS + 1, near[2]),
        copy(qbuf.at[1, c], qbuf.at[1, c], S_Q, near[4]),
        copy(pv.at[other], dbuf.at[c], S_D, near[4]),
        copy(qbuf.at[1, c], qbuf.at[0, c], S_Q + 1, near[0]),
        copy(qbuf.at[1, c], qbuf.at[0, c], S_Q + 2, near[1]),
        copy(qbuf.at[1, c], qbuf.at[2, c], S_Q + 3, near[2]),
        copy(qbuf.at[1, c], qbuf.at[2, c], S_Q + 4, near[3]),
    ]
    for send in sends:
        send.start()
    for device in (at(dz=1), at(dz=-1), at(dy=-1), at(dx=-1), at(dx=1)):
        signal(s1, device)

    fill(k_self, 0, 3)
    fill(k_pair, 1, 0, STRIPS // 2, range(STRIPS // 2))
    fill(k_pair, 1, STRIPS // 2, STRIPS, range(STRIPS // 2, STRIPS))

    def by_tile(group):
        first, second = qbuf[group, 0].astype(F32), qbuf[group, 1].astype(F32)
        return (
            jnp.concatenate([first[:HALF], second[:HALF]], 0),
            jnp.concatenate([first[HALF:], second[HALF:]], 0),
        )

    pl.semaphore_wait(s1, 5)
    for device in (at(dz=2), at(dz=-2), at(dx=-1), at(dx=1)):
        signal(s2, device)
    sends[2].wait_recv()
    t0, t1 = by_tile(1)
    qt[0] = jnp.where(c == 0, t0, t1).astype(BF16)
    qt[1] = in_order(jnp.where(c == 0, t1, t0)).astype(BF16)
    for h in HALVES:
        zp[:, h] = times(qt.at[0, :, h], k_pair.at[h, h])
    zp[...] = in_order(zp[...])
    to_partner = copy(zp, zo, S_T, near[4])
    to_partner.start()
    zf[...] = times(qt.at[0], k_self)
    for h in HALVES:
        zf[:, h] += times_rows(qt.at[1, :, h], k_pair.at[h, h])

    sends[0].wait_recv()
    sends[1].wait_recv()
    loads[2].wait()
    loads[3].wait()
    first_next = 2 * (g + 1)
    low = (pairs[c, 1] >= first_next) | (pairs[c, 2] >= first_next) | (pairs[c, 3] >= first_next)
    lane[2] = jnp.where(low, cbuf[2, c], cbuf[0, other]) * 8.0
    lane[3] = jnp.where(low, cbuf[2, other], cbuf[0, c]) * 8.0
    fill(k_near, 2)

    pl.semaphore_wait(s2, 4)
    for device in (at(dz=4), at(dz=-4), at(dx=-1)):
        signal(s3, device)
    fill(k_far, 3)
    for send in sends[4:]:
        send.wait_recv()
    p0, p1 = by_tile(0)
    n0, n1 = by_tile(2)
    qt[2] = jnp.where(low, jnp.where(c == 0, n0, n1), jnp.where(c == 0, p1, p0)).astype(BF16)
    qt[3] = jnp.where(low, jnp.where(c == 0, n1, n0), jnp.where(c == 0, p0, p1)).astype(BF16)
    sends[3].wait_recv()
    noise_row = nv[pl.ds(c, 1), :]
    start = dbuf[...].reshape(CHIP, PTS)
    to_partner.wait_recv()
    image = zf[...] + zo[...] + times_rows(qt.at[2], k_near) + times_rows(qt.at[3], k_far)
    image = noise_row * start + image * (1.0 / 256.0)
    zf[...] = image
    zb[...] = image.astype(BF16)

    fields = [
        copy(zb, zr.at[1], S_Z, near[2]),
        copy(zb, zr.at[2], S_Z + 1, near[1]),
        copy(zb, zr.at[0], S_Z + 2, near[4]),
        copy(zf.at[pl.ds(pl.multiple_of(other * HALF, HALF), HALF), :], zx, S_ZX, near[4]),
    ]
    for send in fields:
        send.start()
    products = (start * start, start * image)
    for j in range(STRIPS):
        for i in range(2):
            ps[j, i] = products[i][:, j * LANES : (j + 1) * LANES]
    shares = []
    for j, (dx, dc) in enumerate([(dx, dc) for dx in range(NX) for dc in range(2)][1:]):
        device = at(dx=dx, dc=dc)
        shares.append(copy(ps.at[device["probe"]], pr.at[j], S_P, device))
    for send in shares:
        send.start()
    all_shares = copy(pr, pr, S_P, near[4])

    moments = [fold(products[0]), fold(products[1]), fold(image * image)]
    square = fold(image * (times(zb, k_self) * (1.0 / 256.0) + noise_row * image))
    to_near = times(zb, k_near)
    to_pair = jnp.concatenate([times(zb.at[:, h], k_pair.at[h, h]) for h in HALVES], 1)
    pl.semaphore_wait(s3, 3)
    fields[2].wait_recv()
    square = square + fold(to_pair * in_order(zr[0].astype(F32))) * (2.0 / 256.0)
    fields[0].wait_recv()
    fields[1].wait_recv()
    across = jnp.where(low, zr[1].astype(F32), zr[2].astype(F32))
    square = square + fold(to_near * across) * (2.0 / 256.0)

    table = jnp.concatenate(moments + [square, jnp.zeros((64, LANES), F32)], 0)
    az[0] = jnp.sum(table.T, axis=0, keepdims=True)
    along_z = [copy(az.at[0], az.at[i], S_AZ, at(dz=i // 2, dc=i % 2)) for i in range(1, 2 * NZ)]
    all_z = copy(az.at[pl.ds(1, 2 * NZ - 1)], az.at[pl.ds(1, 2 * NZ - 1)], S_AZ, near[4])
    for i in sorted(range(1, 2 * NZ), key=lambda i: -min(i // 2, NZ - i // 2)):
        along_z[i - 1].start()
    for send in sends + fields + [to_partner, all_shares]:
        send.wait_send()
    all_z.wait_recv()
    ay[0] = jnp.sum(az[...], axis=0)
    plane = [copy(ay.at[0], ay.at[i], S_AY, at(dx=i // NY, dy=i % NY)) for i in range(1, NX * NY)]
    for i in sorted(range(1, NX * NY), key=lambda i: -(min(i // NY, NX - i // NY) + min(i % NY, NY - i % NY))):
        plane[i - 1].start()
    all_plane = copy(ay.at[pl.ds(1, NX * NY - 1)], ay.at[pl.ds(1, NX * NY - 1)], S_AY, near[4])
    all_z.wait_send()
    fields[3].wait_recv()
    all_shares.wait_recv()
    all_plane.wait_recv()
    m0 = jnp.concatenate([jnp.sum(ay[NY * i : NY * (i + 1)], axis=0) for i in range(NX)], 0)
    m1, m2, m3 = (pltpu.roll(m0, LANES - CHIP * i, 1) for i in (1, 2, 3))
    step0 = m0 / m1
    growth = m2 / m1
    step1 = (m2 - m1 * m1 / m0) / (m3 - m2 * growth)
    alpha, beta = step0 + step0 * step1 * growth, -step0 * step1
    at_lane = lax.broadcasted_iota(jnp.int32, (1, LANES), 1)
    packed = jnp.zeros((1, LANES), F32)
    for i in range(NX):
        for h, value in enumerate((alpha, beta)):
            first = 32 * i + CHIP * h
            row = value[i : i + 1]
            if first:
                row = pltpu.roll(row, first, 1)
            packed = jnp.where((at_lane >= first) & (at_lane < first + CHIP), row, packed)
    coef[...] = jnp.broadcast_to(packed, (LANES, LANES)).T

    mine = pl.ds(pl.multiple_of(c * HALF, HALF), HALF)
    alpha_mine = jnp.concatenate([coef[mine, :]] * STRIPS, 1)
    beta_mine = jnp.concatenate([coef[pl.ds(pl.multiple_of(CHIP + c * HALF, HALF), HALF), :]] * STRIPS, 1)
    sol[c] = alpha_mine * pv[c] + beta_mine * zf[mine, :]
    sol[other] = alpha_mine * pv[other] + beta_mine * zx[...]
    for dc, tile in ((0, c), (1, other)):
        total = jnp.zeros((CHIP, LANES), F32)
        for dx in range(NX):
            share = ps.at[k] if (dx, dc) == (0, 0) else pr.at[2 * dx + dc - 1]
            total = total + coef[32 * dx : 32 * dx + CHIP, :] * share[0]
            total = total + coef[32 * dx + CHIP : 32 * dx + 2 * CHIP, :] * share[1]
        var[pl.ds(tile, 1), :] = jnp.sum(total, axis=0, keepdims=True) * (1.0 / PROBES)
    all_plane.wait_send()


def shards(coords, noise_var, probes, pair_list):
    anywhere = pl.BlockSpec(memory_space=pl.ANY)
    return pl.pallas_call(
        kernel,
        out_shape=(
            jax.ShapeDtypeStruct(probes.shape, F32),
            jax.ShapeDtypeStruct((2, LANES), F32),
        ),
        in_specs=[anywhere] * 4,
        out_specs=[pl.BlockSpec(memory_space=pltpu.VMEM)] * 2,
        scratch_shapes=[
            pltpu.SMEM((2, 4), jnp.int32),
            pltpu.VMEM((3, 2, 2, PTS), F32),
            pltpu.VMEM((4, 2, PTS), F32),
            pltpu.VMEM((2, PTS, LANES), F32),
            pltpu.VMEM((2, PTS), F32),
            pltpu.VMEM((2, HALF, PTS), F32),
            pltpu.VMEM((3, 2, 2 * HALF, PTS), BF16),
            pltpu.VMEM((2, HALF, PTS), F32),
            pltpu.VMEM((4, CHIP, PTS), BF16),
            pltpu.VMEM((PTS, PTS), BF16),
            pltpu.VMEM((PTS, PTS), BF16),
            pltpu.VMEM((PTS, PTS), BF16),
            pltpu.VMEM((PTS, PTS), BF16),
            pltpu.VMEM((CHIP, PTS), F32),
            pltpu.VMEM((CHIP, PTS), F32),
            pltpu.VMEM((CHIP, PTS), F32),
            pltpu.VMEM((CHIP, PTS), BF16),
            pltpu.VMEM((3, CHIP, PTS), BF16),
            pltpu.VMEM((HALF, PTS), F32),
            pltpu.VMEM((2 * NZ, 1, LANES), F32),
            pltpu.VMEM((NX * NY, 1, LANES), F32),
            pltpu.VMEM((LANES, LANES), F32),
            pltpu.VMEM((8, 2, CHIP, LANES), F32),
            pltpu.VMEM((7, 2, CHIP, LANES), F32),
            pltpu.SemaphoreType.DMA((4,)),
            pltpu.SemaphoreType.DMA((N_SEMS,)),
            pltpu.SemaphoreType.DMA((N_SEMS,)),
            pltpu.SemaphoreType.REGULAR,
            pltpu.SemaphoreType.REGULAR,
            pltpu.SemaphoreType.REGULAR,
        ],
        compiler_params=pltpu.CompilerParams(
            collective_id=0, has_side_effects=True, vmem_limit_bytes=32 << 20
        ),
    )(*(pltpu.with_memory_space_constraint(v, pltpu.MemorySpace.HBM) for v in (coords, noise_var, probes, pair_list)))


def solution(mesh):
    in_specs = (
        P("tiles", None, None),
        P("tiles", None),
        P("tiles", "probe", None),
        P("tiles", None),
    )
    out_specs = (P("tiles", "probe", None), P("tiles", "probe"))
    return jax.shard_map(shards, mesh=mesh, in_specs=in_specs, out_specs=out_specs, check_vma=False)
```

```python
import functools
import jax
import jax.numpy as jnp
from jax import lax
from jax.experimental import pallas as pl
from jax.experimental.pallas import tpu as pltpu
from jax.sharding import PartitionSpec as P

F32 = jnp.float32
BF16 = jnp.bfloat16
MESH = pl.DeviceIdType.MESH

PTS = 1024
PROBES = 64
HALF = 8
CHIP = 16
NY, NZ, NX = 4, 16, 4
GROUPS = NY * NZ
LANES = 128
STRIPS = PTS // LANES
WIDE = 2 * LANES
MID = PTS // 2
HALVES = (slice(0, MID), slice(MID, PTS))

S_COORDS, S_Q, S_D, S_Z, S_ZX, S_P, S_AZ, S_AY, S_T = 0, 2, 7, 8, 11, 12, 13, 14, 15
N_SEMS = 16


def fold(values):
    total = values[:, :LANES]
    for strip in range(1, STRIPS):
        total = total + values[:, strip * LANES : (strip + 1) * LANES]
    return total


def kernel(
    coords, noise, probes, pair_list, sol, var,
    pairs, cbuf, lane, spread, nv, pv, qbuf, dbuf, qt, k_self, k_pair, k_near, k_far, zf, zp, zo, zb, zr, zx,
    az, ay, coef, ps, pr, lsem, ssem, rsem, s1, s2, s3, x1, x2, x3,
):
    g = lax.axis_index("tiles")
    k = lax.axis_index("probe")
    y, z, x, c = g // NZ, lax.rem(g, NZ), k // 2, lax.rem(k, 2)
    other = 1 - c
    after, before = lax.rem(g + 1, GROUPS), lax.rem(g + GROUPS - 1, GROUPS)

    def at(dy=0, dz=0, dx=0, dc=0):
        return {
            "tiles": lax.rem(y + NY + dy, NY) * NZ + lax.rem(z + NZ + dz, NZ),
            "probe": lax.rem(x + NX + dx, NX) * 2 + lax.rem(c + dc, 2),
        }

    def signal(sem, device):
        pl.semaphore_signal(sem, inc=1, device_id=device, device_id_type=MESH)

    def copy(src, dst, index, device):
        return pltpu.make_async_remote_copy(
            src_ref=src, dst_ref=dst, send_sem=ssem.at[index], recv_sem=rsem.at[index],
            device_id=device, device_id_type=MESH,
        )

    loads = [
        pltpu.make_async_copy(src, dst, lsem.at[i])
        for i, (src, dst) in enumerate(((coords, cbuf.at[1]), (probes, pv), (noise, nv), (pair_list, pairs)))
    ]
    for load in loads:
        load.start()

    barrier = pltpu.get_barrier_semaphore()
    near = [
        {"tiles": after, "probe": k}, {"tiles": after, "probe": x * 2 + other},
        {"tiles": before, "probe": k}, {"tiles": before, "probe": x * 2 + other},
        at(dc=1), at(dz=1), at(dz=-1), at(dz=1, dc=1), at(dz=-1, dc=1),
        at(dy=1), at(dy=-1), at(dx=1), at(dx=-1),
    ]
    for device in near:
        signal(barrier, device)

    def in_order(values):
        return jnp.where(c == 0, values, jnp.concatenate([values[:, MID:], values[:, :MID]], 1))

    def fill(block, cols, low=0, high=STRIPS, strips=range(PTS // WIDE)):
        def step(r, carry):
            at_rows = pl.ds(pl.multiple_of(r * LANES, LANES), LANES)
            px = jnp.concatenate([spread[0, at_rows, :]] * 2, 1)
            py = jnp.concatenate([spread[1, at_rows, :]] * 2, 1)
            for b in strips:
                cut = slice(b * WIDE, (b + 1) * WIDE)
                dx = px - lane[cols, 0:1, cut]
                dy = py - lane[cols, 1:2, cut]
                s4 = pltpu.reciprocal(lax.rsqrt(dx * dx + dy * dy), approx=True)
                m = jnp.maximum(4.0 - s4, 0.0)
                m = m * m
                block[at_rows, cut] = ((m * m) * (s4 + 1.0)).astype(BF16)
            return carry

        lax.fori_loop(low, high, step, 0)

    def times_rows(field, block):
        return lax.dot_general(
            field[...], block[...], (((1,), (1,)), ((), ())), preferred_element_type=F32
        )

    def times(field, block):
        return jnp.dot(field[...], block[...], preferred_element_type=F32)

    loads[0].wait()
    loads[1].wait()
    lane[0] = cbuf[1, c] * 8.0
    for axis in range(2):
        for b in range(STRIPS):
            cut = slice(b * LANES, (b + 1) * LANES)
            spread[axis, cut, :] = jnp.broadcast_to(lane[0, axis : axis + 1, cut], (LANES, LANES)).T
    qbuf[1, c] = pv[...].reshape(2 * HALF, PTS).astype(BF16)
    dbuf[c] = pv[c]
    lane[1] = in_order(cbuf[1, other]) * 8.0
    fill(k_self, 0, 0, 3)

    pl.semaphore_wait(barrier, len(near))
    sends = [
        copy(cbuf.at[1], cbuf.at[0], S_COORDS, near[0]),
        copy(cbuf.at[1], cbuf.at[2], S_COORDS + 1, near[2]),
        copy(qbuf.at[1, c], qbuf.at[1, c], S_Q, near[4]),
        copy(pv.at[other], dbuf.at[c], S_D, near[4]),
        copy(qbuf.at[1, c], qbuf.at[0, c], S_Q + 1, near[0]),
        copy(qbuf.at[1, c], qbuf.at[0, c], S_Q + 2, near[1]),
        copy(qbuf.at[1, c], qbuf.at[2, c], S_Q + 3, near[2]),
        copy(qbuf.at[1, c], qbuf.at[2, c], S_Q + 4, near[3]),
    ]
    for send in sends:
        send.start()
    for device in (at(dz=1), at(dz=-1)):
        signal(s1, device)

    fill(k_self, 0, 3)
    fill(k_pair, 1, 0, STRIPS // 2, range(MID // WIDE))
    fill(k_pair, 1, STRIPS // 2, STRIPS, range(MID // WIDE, PTS // WIDE))

    def by_tile(group):
        first, second = qbuf[group, 0].astype(F32), qbuf[group, 1].astype(F32)
        return (
            jnp.concatenate([first[:HALF], second[:HALF]], 0),
            jnp.concatenate([first[HALF:], second[HALF:]], 0),
        )

    pl.semaphore_wait(s1, 2)
    for device in (at(dz=2), at(dz=-2)):
        signal(s2, device)
    sends[2].wait_recv()
    t0, t1 = by_tile(1)
    qt[0] = jnp.where(c == 0, t0, t1).astype(BF16)
    qt[1] = in_order(jnp.where(c == 0, t1, t0)).astype(BF16)
    for h in HALVES:
        zp[:, h] = times(qt.at[0, :, h], k_pair.at[h, h])
    zp[...] = in_order(zp[...])
    to_partner = copy(zp, zo, S_T, near[4])
    to_partner.start()
    zf[...] = times(qt.at[0], k_self)
    for h in HALVES:
        zf[:, h] += times_rows(qt.at[1, :, h], k_pair.at[h, h])

    sends[0].wait_recv()
    sends[1].wait_recv()
    loads[2].wait()
    loads[3].wait()
    first_next = 2 * (g + 1)
    low = (pairs[c, 1] >= first_next) | (pairs[c, 2] >= first_next) | (pairs[c, 3] >= first_next)
    lane[2] = jnp.where(low, cbuf[2, c], cbuf[0, other]) * 8.0
    lane[3] = jnp.where(low, cbuf[2, other], cbuf[0, c]) * 8.0
    fill(k_near, 2)

    pl.semaphore_wait(s2, 2)
    for device in (at(dz=4), at(dz=-4)):
        signal(s3, device)
    fill(k_far, 3)
    for send in sends[4:]:
        send.wait_recv()
    p0, p1 = by_tile(0)
    n0, n1 = by_tile(2)
    qt[2] = jnp.where(low, jnp.where(c == 0, n0, n1), jnp.where(c == 0, p1, p0)).astype(BF16)
    qt[3] = jnp.where(low, jnp.where(c == 0, n1, n0), jnp.where(c == 0, p0, p1)).astype(BF16)
    sends[3].wait_recv()
    noise_row = nv[pl.ds(c, 1), :]
    start = dbuf[...].reshape(CHIP, PTS)
    to_partner.wait_recv()
    image = zf[...] + zo[...] + times_rows(qt.at[2], k_near) + times_rows(qt.at[3], k_far)
    image = noise_row * start + image * (1.0 / 256.0)
    zf[...] = image
    zb[...] = image.astype(BF16)

    fields = [
        copy(zb, zr.at[1], S_Z, near[2]),
        copy(zb, zr.at[2], S_Z + 1, near[1]),
        copy(zb, zr.at[0], S_Z + 2, near[4]),
        copy(zf.at[pl.ds(pl.multiple_of(other * HALF, HALF), HALF), :], zx, S_ZX, near[4]),
    ]
    for send in fields[:3]:
        send.start()
    for device in (at(dy=-1), at(dx=-1), at(dx=1)):
        signal(x1, device)
    products = (start * start, start * image)
    moments = [fold(products[0]), fold(products[1]), fold(image * image)]
    square = fold(image * (times(zb, k_self) * (1.0 / 256.0) + noise_row * image))
    to_near = times(zb, k_near)
    to_pair = jnp.concatenate([times(zb.at[:, h], k_pair.at[h, h]) for h in HALVES], 1)
    pl.semaphore_wait(s3, 2)
    fields[2].wait_recv()
    square = square + fold(to_pair * in_order(zr[0].astype(F32))) * (2.0 / 256.0)
    fields[0].wait_recv()
    fields[1].wait_recv()
    across = jnp.where(low, zr[1].astype(F32), zr[2].astype(F32))
    square = square + fold(to_near * across) * (2.0 / 256.0)

    table = jnp.concatenate(moments + [square, jnp.zeros((64, LANES), F32)], 0)
    az[0] = jnp.sum(table.T, axis=0, keepdims=True)
    along_z = [copy(az.at[0], az.at[i], S_AZ, at(dz=i // 2, dc=i % 2)) for i in range(1, 2 * NZ)]
    all_z = copy(az.at[pl.ds(1, 2 * NZ - 1)], az.at[pl.ds(1, 2 * NZ - 1)], S_AZ, near[4])
    for i in sorted(range(1, 2 * NZ), key=lambda i: -min(i // 2, NZ - i // 2)):
        along_z[i - 1].start()
    pl.semaphore_wait(x1, 3)
    for device in (at(dx=-1), at(dx=1)):
        signal(x2, device)
    for j in range(STRIPS):
        for i in range(2):
            ps[j, i] = products[i][:, j * LANES : (j + 1) * LANES]
    fields[3].start()
    pl.semaphore_wait(x2, 2)
    signal(x3, at(dx=-1))
    shares = []
    for j, (dx, dc) in enumerate([(dx, dc) for dx in range(NX) for dc in range(2)][1:]):
        device = at(dx=dx, dc=dc)
        shares.append(copy(ps.at[device["probe"]], pr.at[j], S_P, device))
    for send in shares:
        send.start()
    all_shares = copy(pr, pr, S_P, near[4])

    for send in sends + fields + [to_partner, all_shares]:
        send.wait_send()
    pl.semaphore_wait(x3, 1)
    all_z.wait_recv()
    ay[0] = jnp.sum(az[...], axis=0)
    plane = [copy(ay.at[0], ay.at[i], S_AY, at(dx=i // NY, dy=i % NY)) for i in range(1, NX * NY)]
    for i in sorted(range(1, NX * NY), key=lambda i: -(min(i // NY, NX - i // NY) + min(i % NY, NY - i % NY))):
        plane[i - 1].start()
    all_plane = copy(ay.at[pl.ds(1, NX * NY - 1)], ay.at[pl.ds(1, NX * NY - 1)], S_AY, near[4])
    all_z.wait_send()
    fields[3].wait_recv()
    all_shares.wait_recv()
    all_plane.wait_recv()
    m0 = jnp.concatenate([jnp.sum(ay[NY * i : NY * (i + 1)], axis=0) for i in range(NX)], 0)
    m1, m2, m3 = (pltpu.roll(m0, LANES - CHIP * i, 1) for i in (1, 2, 3))
    step0 = m0 / m1
    growth = m2 / m1
    step1 = (m2 - m1 * m1 / m0) / (m3 - m2 * growth)
    alpha, beta = step0 + step0 * step1 * growth, -step0 * step1
    at_lane = lax.broadcasted_iota(jnp.int32, (1, LANES), 1)
    packed = jnp.zeros((1, LANES), F32)
    for i in range(NX):
        for h, value in enumerate((alpha, beta)):
            first = 32 * i + CHIP * h
            row = value[i : i + 1]
            if first:
                row = pltpu.roll(row, first, 1)
            packed = jnp.where((at_lane >= first) & (at_lane < first + CHIP), row, packed)
    coef[...] = jnp.broadcast_to(packed, (LANES, LANES)).T

    mine = pl.ds(pl.multiple_of(c * HALF, HALF), HALF)
    alpha_mine = jnp.concatenate([coef[mine, :]] * STRIPS, 1)
    beta_mine = jnp.concatenate([coef[pl.ds(pl.multiple_of(CHIP + c * HALF, HALF), HALF), :]] * STRIPS, 1)
    sol[c] = alpha_mine * pv[c] + beta_mine * zf[mine, :]
    sol[other] = alpha_mine * pv[other] + beta_mine * zx[...]
    for dc, tile in ((0, c), (1, other)):
        total = jnp.zeros((CHIP, LANES), F32)
        for dx in range(NX):
            share = ps.at[k] if (dx, dc) == (0, 0) else pr.at[2 * dx + dc - 1]
            total = total + coef[32 * dx : 32 * dx + CHIP, :] * share[0]
            total = total + coef[32 * dx + CHIP : 32 * dx + 2 * CHIP, :] * share[1]
        var[pl.ds(tile, 1), :] = jnp.sum(total, axis=0, keepdims=True) * (1.0 / PROBES)
    all_plane.wait_send()


def shards(coords, noise_var, probes, pair_list):
    anywhere = pl.BlockSpec(memory_space=pl.ANY)
    return pl.pallas_call(
        kernel,
        out_shape=(
            jax.ShapeDtypeStruct(probes.shape, F32),
            jax.ShapeDtypeStruct((2, LANES), F32),
        ),
        in_specs=[anywhere] * 4,
        out_specs=[pl.BlockSpec(memory_space=pltpu.VMEM)] * 2,
        scratch_shapes=[
            pltpu.SMEM((2, 4), jnp.int32),
            pltpu.VMEM((3, 2, 2, PTS), F32),
            pltpu.VMEM((4, 2, PTS), F32),
            pltpu.VMEM((2, PTS, LANES), F32),
            pltpu.VMEM((2, PTS), F32),
            pltpu.VMEM((2, HALF, PTS), F32),
            pltpu.VMEM((3, 2, 2 * HALF, PTS), BF16),
            pltpu.VMEM((2, HALF, PTS), F32),
            pltpu.VMEM((4, CHIP, PTS), BF16),
            pltpu.VMEM((PTS, PTS), BF16),
            pltpu.VMEM((PTS, PTS), BF16),
            pltpu.VMEM((PTS, PTS), BF16),
            pltpu.VMEM((PTS, PTS), BF16),
            pltpu.VMEM((CHIP, PTS), F32),
            pltpu.VMEM((CHIP, PTS), F32),
            pltpu.VMEM((CHIP, PTS), F32),
            pltpu.VMEM((CHIP, PTS), BF16),
            pltpu.VMEM((3, CHIP, PTS), BF16),
            pltpu.VMEM((HALF, PTS), F32),
            pltpu.VMEM((2 * NZ, 1, LANES), F32),
            pltpu.VMEM((NX * NY, 1, LANES), F32),
            pltpu.VMEM((LANES, LANES), F32),
            pltpu.VMEM((8, 2, CHIP, LANES), F32),
            pltpu.VMEM((7, 2, CHIP, LANES), F32),
            pltpu.SemaphoreType.DMA((4,)),
            pltpu.SemaphoreType.DMA((N_SEMS,)),
            pltpu.SemaphoreType.DMA((N_SEMS,)),
            pltpu.SemaphoreType.REGULAR,
            pltpu.SemaphoreType.REGULAR,
            pltpu.SemaphoreType.REGULAR,
            pltpu.SemaphoreType.REGULAR,
            pltpu.SemaphoreType.REGULAR,
            pltpu.SemaphoreType.REGULAR,
        ],
        compiler_params=pltpu.CompilerParams(
            collective_id=0, has_side_effects=True, vmem_limit_bytes=32 << 20
        ),
    )(*(pltpu.with_memory_space_constraint(v, pltpu.MemorySpace.HBM) for v in (coords, noise_var, probes, pair_list)))


def solution(mesh):
    in_specs = (
        P("tiles", None, None),
        P("tiles", None),
        P("tiles", "probe", None),
        P("tiles", None),
    )
    out_specs = (P("tiles", "probe", None), P("tiles", "probe"))
    return jax.shard_map(shards, mesh=mesh, in_specs=in_specs, out_specs=out_specs, check_vma=False)
```

```python
import functools
import jax
import jax.numpy as jnp
from jax import lax
from jax.experimental import pallas as pl
from jax.experimental.pallas import tpu as pltpu
from jax.sharding import PartitionSpec as P

F32 = jnp.float32
BF16 = jnp.bfloat16
MESH = pl.DeviceIdType.MESH

PTS = 1024
PROBES = 64
HALF = 8
CHIP = 16
NY, NZ, NX = 4, 16, 4
GROUPS = NY * NZ
LANES = 128
STRIPS = PTS // LANES
WIDE = 2 * LANES
BAND = 256
BANDS = PTS // BAND
MID = PTS // 2
HALVES = (slice(0, MID), slice(MID, PTS))

S_COORDS, S_Q, S_D, S_Z, S_ZX, S_P, S_AZ, S_AY, S_T = 0, 2, 7, 8, 11, 12, 13, 14, 15
N_SEMS = 16


def fold(values):
    total = values[:, :LANES]
    for strip in range(1, STRIPS):
        total = total + values[:, strip * LANES : (strip + 1) * LANES]
    return total


def kernel(
    coords, noise, probes, pair_list, sol, var,
    pairs, cbuf, lane, spread, nv, pv, qbuf, dbuf, qt, k_self, k_pair, k_near, k_far, zf, zp, zo, zb, zr, zx,
    az, ay, coef, ps, pr, lsem, ssem, rsem, s1, s2, s3, x1, x2, x3,
):
    g = lax.axis_index("tiles")
    k = lax.axis_index("probe")
    y, z, x, c = g // NZ, lax.rem(g, NZ), k // 2, lax.rem(k, 2)
    other = 1 - c
    after, before = lax.rem(g + 1, GROUPS), lax.rem(g + GROUPS - 1, GROUPS)

    def at(dy=0, dz=0, dx=0, dc=0):
        return {
            "tiles": lax.rem(y + NY + dy, NY) * NZ + lax.rem(z + NZ + dz, NZ),
            "probe": lax.rem(x + NX + dx, NX) * 2 + lax.rem(c + dc, 2),
        }

    def signal(sem, device):
        pl.semaphore_signal(sem, inc=1, device_id=device, device_id_type=MESH)

    def copy(src, dst, index, device):
        return pltpu.make_async_remote_copy(
            src_ref=src, dst_ref=dst, send_sem=ssem.at[index], recv_sem=rsem.at[index],
            device_id=device, device_id_type=MESH,
        )

    loads = [
        pltpu.make_async_copy(src, dst, lsem.at[i])
        for i, (src, dst) in enumerate(((coords, cbuf.at[1]), (probes, pv), (noise, nv), (pair_list, pairs)))
    ]
    for load in loads:
        load.start()

    barrier = pltpu.get_barrier_semaphore()
    near = [
        {"tiles": after, "probe": k}, {"tiles": after, "probe": x * 2 + other},
        {"tiles": before, "probe": k}, {"tiles": before, "probe": x * 2 + other},
        at(dc=1), at(dz=1), at(dz=-1), at(dz=1, dc=1), at(dz=-1, dc=1),
        at(dy=1), at(dy=-1), at(dx=1), at(dx=-1),
    ]
    for device in near:
        signal(barrier, device)

    def in_order(values):
        return jnp.where(c == 0, values, jnp.concatenate([values[:, MID:], values[:, :MID]], 1))

    def fill(block, cols, low=0, high=BANDS, strips=range(PTS // WIDE)):
        def step(r, carry):
            at_rows = pl.ds(pl.multiple_of(r * BAND, BAND), BAND)
            px = jnp.concatenate([spread[0, at_rows, :]] * 2, 1)
            py = jnp.concatenate([spread[1, at_rows, :]] * 2, 1)
            for b in strips:
                cut = slice(b * WIDE, (b + 1) * WIDE)
                dx = px - lane[cols, 0:1, cut]
                dy = py - lane[cols, 1:2, cut]
                s4 = pltpu.reciprocal(lax.rsqrt(dx * dx + dy * dy), approx=True)
                m = jnp.maximum(4.0 - s4, 0.0)
                m = m * m
                block[at_rows, cut] = ((m * m) * (s4 + 1.0)).astype(BF16)
            return carry

        lax.fori_loop(low, high, step, 0)

    def times_rows(field, block):
        return lax.dot_general(
            field[...], block[...], (((1,), (1,)), ((), ())), preferred_element_type=F32
        )

    def times(field, block):
        return jnp.dot(field[...], block[...], preferred_element_type=F32)

    loads[0].wait()
    loads[1].wait()
    lane[0] = cbuf[1, c] * 8.0
    for axis in range(2):
        for b in range(STRIPS):
            cut = slice(b * LANES, (b + 1) * LANES)
            spread[axis, cut, :] = jnp.broadcast_to(lane[0, axis : axis + 1, cut], (LANES, LANES)).T
    qbuf[1, c] = pv[...].reshape(2 * HALF, PTS).astype(BF16)
    dbuf[c] = pv[c]
    lane[1] = in_order(cbuf[1, other]) * 8.0
    fill(k_self, 0, 0, 1)

    pl.semaphore_wait(barrier, len(near))
    sends = [
        copy(cbuf.at[1], cbuf.at[0], S_COORDS, near[0]),
        copy(cbuf.at[1], cbuf.at[2], S_COORDS + 1, near[2]),
        copy(qbuf.at[1, c], qbuf.at[1, c], S_Q, near[4]),
        copy(pv.at[other], dbuf.at[c], S_D, near[4]),
        copy(qbuf.at[1, c], qbuf.at[0, c], S_Q + 1, near[0]),
        copy(qbuf.at[1, c], qbuf.at[0, c], S_Q + 2, near[1]),
        copy(qbuf.at[1, c], qbuf.at[2, c], S_Q + 3, near[2]),
        copy(qbuf.at[1, c], qbuf.at[2, c], S_Q + 4, near[3]),
    ]
    for send in sends[:4]:
        send.start()
    for device in (at(dz=1), at(dz=-1)):
        signal(s1, device)

    fill(k_self, 0, 1)
    for send in sends[4:]:
        send.start()
    fill(k_pair, 1, 0, BANDS // 2, range(MID // WIDE))
    fill(k_pair, 1, BANDS // 2, BANDS, range(MID // WIDE, PTS // WIDE))

    def by_tile(group):
        first, second = qbuf[group, 0].astype(F32), qbuf[group, 1].astype(F32)
        return (
            jnp.concatenate([first[:HALF], second[:HALF]], 0),
            jnp.concatenate([first[HALF:], second[HALF:]], 0),
        )

    pl.semaphore_wait(s1, 2)
    for device in (at(dz=2), at(dz=-2)):
        signal(s2, device)
    sends[2].wait_recv()
    t0, t1 = by_tile(1)
    qt[0] = jnp.where(c == 0, t0, t1).astype(BF16)
    qt[1] = in_order(jnp.where(c == 0, t1, t0)).astype(BF16)
    for h in HALVES:
        zp[:, h] = times(qt.at[0, :, h], k_pair.at[h, h])
    zp[...] = in_order(zp[...])
    to_partner = copy(zp, zo, S_T, near[4])
    to_partner.start()
    zf[...] = times(qt.at[0], k_self)
    for h in HALVES:
        zf[:, h] += times_rows(qt.at[1, :, h], k_pair.at[h, h])

    sends[0].wait_recv()
    sends[1].wait_recv()
    loads[2].wait()
    loads[3].wait()
    first_next = 2 * (g + 1)
    low = (pairs[c, 1] >= first_next) | (pairs[c, 2] >= first_next) | (pairs[c, 3] >= first_next)
    lane[2] = jnp.where(low, cbuf[2, c], cbuf[0, other]) * 8.0
    lane[3] = jnp.where(low, cbuf[2, other], cbuf[0, c]) * 8.0
    fill(k_near, 2)

    pl.semaphore_wait(s2, 2)
    for device in (at(dz=4), at(dz=-4)):
        signal(s3, device)
    fill(k_far, 3)
    for send in sends[4:]:
        send.wait_recv()
    p0, p1 = by_tile(0)
    n0, n1 = by_tile(2)
    qt[2] = jnp.where(low, jnp.where(c == 0, n0, n1), jnp.where(c == 0, p1, p0)).astype(BF16)
    qt[3] = jnp.where(low, jnp.where(c == 0, n1, n0), jnp.where(c == 0, p0, p1)).astype(BF16)
    sends[3].wait_recv()
    noise_row = nv[pl.ds(c, 1), :]
    start = dbuf[...].reshape(CHIP, PTS)
    to_partner.wait_recv()
    image = zf[...] + zo[...] + times_rows(qt.at[2], k_near) + times_rows(qt.at[3], k_far)
    image = noise_row * start + image * (1.0 / 256.0)
    zf[...] = image
    zb[...] = image.astype(BF16)

    fields = [
        copy(zb, zr.at[1], S_Z, near[2]),
        copy(zb, zr.at[2], S_Z + 1, near[1]),
        copy(zb, zr.at[0], S_Z + 2, near[4]),
        copy(zf.at[pl.ds(pl.multiple_of(other * HALF, HALF), HALF), :], zx, S_ZX, near[4]),
    ]
    for send in fields[:3]:
        send.start()
    for device in (at(dy=-1), at(dx=-1), at(dx=1)):
        signal(x1, device)
    products = (start * start, start * image)
    moments = [fold(products[0]), fold(products[1]), fold(image * image)]
    square = fold(image * (times(zb, k_self) * (1.0 / 256.0) + noise_row * image))
    to_near = times(zb, k_near)
    to_pair = jnp.concatenate([times(zb.at[:, h], k_pair.at[h, h]) for h in HALVES], 1)
    pl.semaphore_wait(s3, 2)
    fields[2].wait_recv()
    square = square + fold(to_pair * in_order(zr[0].astype(F32))) * (2.0 / 256.0)
    fields[0].wait_recv()
    fields[1].wait_recv()
    across = jnp.where(low, zr[1].astype(F32), zr[2].astype(F32))
    square = square + fold(to_near * across) * (2.0 / 256.0)

    table = jnp.concatenate(moments + [square, jnp.zeros((64, LANES), F32)], 0)
    az[0] = jnp.sum(table.T, axis=0, keepdims=True)
    along_z = [copy(az.at[0], az.at[i], S_AZ, at(dz=i // 2, dc=i % 2)) for i in range(1, 2 * NZ)]
    all_z = copy(az.at[pl.ds(1, 2 * NZ - 1)], az.at[pl.ds(1, 2 * NZ - 1)], S_AZ, near[4])
    for i in sorted(range(1, 2 * NZ), key=lambda i: -min(i // 2, NZ - i // 2)):
        along_z[i - 1].start()
    pl.semaphore_wait(x1, 3)
    for device in (at(dx=-1), at(dx=1)):
        signal(x2, device)
    for j in range(STRIPS):
        for i in range(2):
            ps[j, i] = products[i][:, j * LANES : (j + 1) * LANES]
    fields[3].start()
    pl.semaphore_wait(x2, 2)
    signal(x3, at(dx=-1))
    shares = []
    for j, (dx, dc) in enumerate([(dx, dc) for dx in range(NX) for dc in range(2)][1:]):
        device = at(dx=dx, dc=dc)
        shares.append(copy(ps.at[device["probe"]], pr.at[j], S_P, device))
    for send in shares:
        send.start()
    all_shares = copy(pr, pr, S_P, near[4])

    for send in sends + fields + [to_partner, all_shares]:
        send.wait_send()
    pl.semaphore_wait(x3, 1)
    all_z.wait_recv()
    ay[0] = jnp.sum(az[...], axis=0)
    plane = [copy(ay.at[0], ay.at[i], S_AY, at(dx=i // NY, dy=i % NY)) for i in range(1, NX * NY)]
    for i in sorted(range(1, NX * NY), key=lambda i: -(min(i // NY, NX - i // NY) + min(i % NY, NY - i % NY))):
        plane[i - 1].start()
    all_plane = copy(ay.at[pl.ds(1, NX * NY - 1)], ay.at[pl.ds(1, NX * NY - 1)], S_AY, near[4])
    all_z.wait_send()
    fields[3].wait_recv()
    all_shares.wait_recv()
    all_plane.wait_recv()
    m0 = jnp.concatenate([jnp.sum(ay[NY * i : NY * (i + 1)], axis=0) for i in range(NX)], 0)
    m1, m2, m3 = (pltpu.roll(m0, LANES - CHIP * i, 1) for i in (1, 2, 3))
    step0 = m0 / m1
    growth = m2 / m1
    step1 = (m2 - m1 * m1 / m0) / (m3 - m2 * growth)
    alpha, beta = step0 + step0 * step1 * growth, -step0 * step1
    at_lane = lax.broadcasted_iota(jnp.int32, (1, LANES), 1)
    packed = jnp.zeros((1, LANES), F32)
    for i in range(NX):
        for h, value in enumerate((alpha, beta)):
            first = 32 * i + CHIP * h
            row = value[i : i + 1]
            if first:
                row = pltpu.roll(row, first, 1)
            packed = jnp.where((at_lane >= first) & (at_lane < first + CHIP), row, packed)
    coef[...] = jnp.broadcast_to(packed, (LANES, LANES)).T

    mine = pl.ds(pl.multiple_of(c * HALF, HALF), HALF)
    alpha_mine = jnp.concatenate([coef[mine, :]] * STRIPS, 1)
    beta_mine = jnp.concatenate([coef[pl.ds(pl.multiple_of(CHIP + c * HALF, HALF), HALF), :]] * STRIPS, 1)
    sol[c] = alpha_mine * pv[c] + beta_mine * zf[mine, :]
    sol[other] = alpha_mine * pv[other] + beta_mine * zx[...]
    for dc, tile in ((0, c), (1, other)):
        total = jnp.zeros((CHIP, LANES), F32)
        for dx in range(NX):
            share = ps.at[k] if (dx, dc) == (0, 0) else pr.at[2 * dx + dc - 1]
            total = total + coef[32 * dx : 32 * dx + CHIP, :] * share[0]
            total = total + coef[32 * dx + CHIP : 32 * dx + 2 * CHIP, :] * share[1]
        var[pl.ds(tile, 1), :] = jnp.sum(total, axis=0, keepdims=True) * (1.0 / PROBES)
    all_plane.wait_send()


def shards(coords, noise_var, probes, pair_list):
    anywhere = pl.BlockSpec(memory_space=pl.ANY)
    return pl.pallas_call(
        kernel,
        out_shape=(
            jax.ShapeDtypeStruct(probes.shape, F32),
            jax.ShapeDtypeStruct((2, LANES), F32),
        ),
        in_specs=[anywhere] * 4,
        out_specs=[pl.BlockSpec(memory_space=pltpu.VMEM)] * 2,
        scratch_shapes=[
            pltpu.SMEM((2, 4), jnp.int32),
            pltpu.VMEM((3, 2, 2, PTS), F32),
            pltpu.VMEM((4, 2, PTS), F32),
            pltpu.VMEM((2, PTS, LANES), F32),
            pltpu.VMEM((2, PTS), F32),
            pltpu.VMEM((2, HALF, PTS), F32),
            pltpu.VMEM((3, 2, 2 * HALF, PTS), BF16),
            pltpu.VMEM((2, HALF, PTS), F32),
            pltpu.VMEM((4, CHIP, PTS), BF16),
            pltpu.VMEM((PTS, PTS), BF16),
            pltpu.VMEM((PTS, PTS), BF16),
            pltpu.VMEM((PTS, PTS), BF16),
            pltpu.VMEM((PTS, PTS), BF16),
            pltpu.VMEM((CHIP, PTS), F32),
            pltpu.VMEM((CHIP, PTS), F32),
            pltpu.VMEM((CHIP, PTS), F32),
            pltpu.VMEM((CHIP, PTS), BF16),
            pltpu.VMEM((3, CHIP, PTS), BF16),
            pltpu.VMEM((HALF, PTS), F32),
            pltpu.VMEM((2 * NZ, 1, LANES), F32),
            pltpu.VMEM((NX * NY, 1, LANES), F32),
            pltpu.VMEM((LANES, LANES), F32),
            pltpu.VMEM((8, 2, CHIP, LANES), F32),
            pltpu.VMEM((7, 2, CHIP, LANES), F32),
            pltpu.SemaphoreType.DMA((4,)),
            pltpu.SemaphoreType.DMA((N_SEMS,)),
            pltpu.SemaphoreType.DMA((N_SEMS,)),
            pltpu.SemaphoreType.REGULAR,
            pltpu.SemaphoreType.REGULAR,
            pltpu.SemaphoreType.REGULAR,
            pltpu.SemaphoreType.REGULAR,
            pltpu.SemaphoreType.REGULAR,
            pltpu.SemaphoreType.REGULAR,
        ],
        compiler_params=pltpu.CompilerParams(
            collective_id=0, has_side_effects=True, vmem_limit_bytes=32 << 20
        ),
    )(*(pltpu.with_memory_space_constraint(v, pltpu.MemorySpace.HBM) for v in (coords, noise_var, probes, pair_list)))


def solution(mesh):
    in_specs = (
        P("tiles", None, None),
        P("tiles", None),
        P("tiles", "probe", None),
        P("tiles", None),
    )
    out_specs = (P("tiles", "probe", None), P("tiles", "probe"))
    return jax.shard_map(shards, mesh=mesh, in_specs=in_specs, out_specs=out_specs, check_vma=False)
```

```python
import functools
import jax
import jax.numpy as jnp
from jax import lax
from jax.experimental import pallas as pl
from jax.experimental.pallas import tpu as pltpu
from jax.sharding import PartitionSpec as P

F32 = jnp.float32
BF16 = jnp.bfloat16
MESH = pl.DeviceIdType.MESH

PTS = 1024
PROBES = 64
HALF = 8
CHIP = 16
NY, NZ, NX = 4, 16, 4
GROUPS = NY * NZ
LANES = 128
STRIPS = PTS // LANES
WIDE = 2 * LANES
BAND = 256
BANDS = PTS // BAND
MID = PTS // 2
HALVES = (slice(0, MID), slice(MID, PTS))

S_COORDS, S_Q, S_D, S_Z, S_ZX, S_P, S_AZ, S_AY, S_T = 0, 2, 7, 8, 11, 12, 13, 14, 15
N_SEMS = 16


def fold(values):
    total = values[:, :LANES]
    for strip in range(1, STRIPS):
        total = total + values[:, strip * LANES : (strip + 1) * LANES]
    return total


def kernel(
    coords, noise, probes, pair_list, sol, var,
    pairs, cbuf, lane, spread, nv, pv, qbuf, dbuf, qt, k_self, k_pair, k_nb, qn, zf, zp, zo, zb, zr, zx,
    az, ay, coef, ps, pr, lsem, ssem, rsem, s1, s2, s3, x1, x2, x3,
):
    g = lax.axis_index("tiles")
    k = lax.axis_index("probe")
    y, z, x, c = g // NZ, lax.rem(g, NZ), k // 2, lax.rem(k, 2)
    other = 1 - c
    after, before = lax.rem(g + 1, GROUPS), lax.rem(g + GROUPS - 1, GROUPS)

    def at(dy=0, dz=0, dx=0, dc=0):
        return {
            "tiles": lax.rem(y + NY + dy, NY) * NZ + lax.rem(z + NZ + dz, NZ),
            "probe": lax.rem(x + NX + dx, NX) * 2 + lax.rem(c + dc, 2),
        }

    def signal(sem, device):
        pl.semaphore_signal(sem, inc=1, device_id=device, device_id_type=MESH)

    def copy(src, dst, index, device):
        return pltpu.make_async_remote_copy(
            src_ref=src, dst_ref=dst, send_sem=ssem.at[index], recv_sem=rsem.at[index],
            device_id=device, device_id_type=MESH,
        )

    loads = [
        pltpu.make_async_copy(src, dst, lsem.at[i])
        for i, (src, dst) in enumerate(((coords, cbuf.at[1]), (probes, pv), (noise, nv), (pair_list, pairs)))
    ]
    for load in loads:
        load.start()

    barrier = pltpu.get_barrier_semaphore()
    near = [
        {"tiles": after, "probe": k}, {"tiles": after, "probe": x * 2 + other},
        {"tiles": before, "probe": k}, {"tiles": before, "probe": x * 2 + other},
        at(dc=1), at(dz=1), at(dz=-1), at(dz=1, dc=1), at(dz=-1, dc=1),
        at(dy=1), at(dy=-1), at(dx=1), at(dx=-1),
    ]
    for device in near:
        signal(barrier, device)

    def in_order(values):
        return jnp.where(c == 0, values, jnp.concatenate([values[:, MID:], values[:, :MID]], 1))

    def fill(block, cols, low=0, high=BANDS, strips=range(PTS // WIDE)):
        def step(r, carry):
            at_rows = pl.ds(pl.multiple_of(r * BAND, BAND), BAND)
            px = jnp.concatenate([spread[0, at_rows, :]] * 2, 1)
            py = jnp.concatenate([spread[1, at_rows, :]] * 2, 1)
            for b in strips:
                cut = slice(b * WIDE, (b + 1) * WIDE)
                dx = px - lane[cols, 0:1, cut]
                dy = py - lane[cols, 1:2, cut]
                s4 = pltpu.reciprocal(lax.rsqrt(dx * dx + dy * dy), approx=True)
                m = jnp.maximum(4.0 - s4, 0.0)
                m = m * m
                block[at_rows, cut] = ((m * m) * (s4 + 1.0)).astype(BF16)
            return carry

        lax.fori_loop(low, high, step, 0)

    def times_rows(field, block):
        return lax.dot_general(
            field[...], block[...], (((1,), (1,)), ((), ())), preferred_element_type=F32
        )

    def times(field, block):
        return jnp.dot(field[...], block[...], preferred_element_type=F32)

    loads[0].wait()
    loads[1].wait()
    lane[0] = cbuf[1, c] * 8.0
    for axis in range(2):
        for b in range(STRIPS):
            cut = slice(b * LANES, (b + 1) * LANES)
            spread[axis, cut, :] = jnp.broadcast_to(lane[0, axis : axis + 1, cut], (LANES, LANES)).T
    qbuf[1, c] = pv[...].reshape(2 * HALF, PTS).astype(BF16)
    dbuf[c] = pv[c]
    lane[1] = in_order(cbuf[1, other]) * 8.0
    fill(k_self, 0, 0, 1)

    pl.semaphore_wait(barrier, len(near))
    sends = [
        copy(cbuf.at[1], cbuf.at[0], S_COORDS, near[0]),
        copy(cbuf.at[1], cbuf.at[2], S_COORDS + 1, near[2]),
        copy(qbuf.at[1, c], qbuf.at[1, c], S_Q, near[4]),
        copy(pv.at[other], dbuf.at[c], S_D, near[4]),
        copy(qbuf.at[1, c], qbuf.at[0, c], S_Q + 1, near[0]),
        copy(qbuf.at[1, c], qbuf.at[0, c], S_Q + 2, near[1]),
        copy(qbuf.at[1, c], qbuf.at[2, c], S_Q + 3, near[2]),
        copy(qbuf.at[1, c], qbuf.at[2, c], S_Q + 4, near[3]),
    ]
    for send in sends[:4]:
        send.start()
    for device in (at(dz=1), at(dz=-1)):
        signal(s1, device)

    fill(k_self, 0, 1)
    for send in sends[4:]:
        send.start()
    fill(k_pair, 1, 0, BANDS // 2, range(MID // WIDE))
    fill(k_pair, 1, BANDS // 2, BANDS, range(MID // WIDE, PTS // WIDE))

    def by_tile(group):
        first, second = qbuf[group, 0].astype(F32), qbuf[group, 1].astype(F32)
        return (
            jnp.concatenate([first[:HALF], second[:HALF]], 0),
            jnp.concatenate([first[HALF:], second[HALF:]], 0),
        )

    pl.semaphore_wait(s1, 2)
    for device in (at(dz=2), at(dz=-2)):
        signal(s2, device)
    sends[2].wait_recv()
    t0, t1 = by_tile(1)
    qt[0] = jnp.where(c == 0, t0, t1).astype(BF16)
    qt[1] = in_order(jnp.where(c == 0, t1, t0)).astype(BF16)
    for h in HALVES:
        zp[:, h] = times(qt.at[0, :, h], k_pair.at[h, h])
    zp[...] = in_order(zp[...])
    to_partner = copy(zp, zo, S_T, near[4])
    to_partner.start()
    zf[...] = times(qt.at[0], k_self)
    for h in HALVES:
        zf[:, h] += times_rows(qt.at[1, :, h], k_pair.at[h, h])

    sends[0].wait_recv()
    sends[1].wait_recv()
    loads[2].wait()
    loads[3].wait()
    first_next = 2 * (g + 1)
    low = (pairs[c, 1] >= first_next) | (pairs[c, 2] >= first_next) | (pairs[c, 3] >= first_next)
    lane[2] = jnp.where(low, cbuf[2, c], cbuf[0, other]) * 8.0
    lane[3] = jnp.where(low, cbuf[2, other], cbuf[0, c]) * 8.0
    k_near, k_far = k_nb.at[:, :PTS], k_nb.at[:, PTS:]
    fill(k_near, 2)

    pl.semaphore_wait(s2, 2)
    for device in (at(dz=4), at(dz=-4)):
        signal(s3, device)
    fill(k_far, 3)
    for send in sends[4:]:
        send.wait_recv()
    p0, p1 = by_tile(0)
    n0, n1 = by_tile(2)
    qn[:, :PTS] = jnp.where(low, jnp.where(c == 0, n0, n1), jnp.where(c == 0, p1, p0)).astype(BF16)
    qn[:, PTS:] = jnp.where(low, jnp.where(c == 0, n1, n0), jnp.where(c == 0, p0, p1)).astype(BF16)
    sends[3].wait_recv()
    noise_row = nv[pl.ds(c, 1), :]
    start = dbuf[...].reshape(CHIP, PTS)
    to_partner.wait_recv()
    image = zf[...] + zo[...] + times_rows(qn, k_nb)
    image = noise_row * start + image * (1.0 / 256.0)
    zf[...] = image
    zb[...] = image.astype(BF16)

    fields = [
        copy(zb, zr.at[1], S_Z, near[2]),
        copy(zb, zr.at[2], S_Z + 1, near[1]),
        copy(zb, zr.at[0], S_Z + 2, near[4]),
        copy(zf.at[pl.ds(pl.multiple_of(other * HALF, HALF), HALF), :], zx, S_ZX, near[4]),
    ]
    for send in fields[:3]:
        send.start()
    for device in (at(dy=-1), at(dx=-1), at(dx=1)):
        signal(x1, device)
    products = (start * start, start * image)
    moments = [fold(products[0]), fold(products[1]), fold(image * image)]
    square = fold(image * (times(zb, k_self) * (1.0 / 256.0) + noise_row * image))
    to_near = times(zb, k_near)
    to_pair = jnp.concatenate([times(zb.at[:, h], k_pair.at[h, h]) for h in HALVES], 1)
    pl.semaphore_wait(s3, 2)
    fields[2].wait_recv()
    square = square + fold(to_pair * in_order(zr[0].astype(F32))) * (2.0 / 256.0)
    fields[0].wait_recv()
    fields[1].wait_recv()
    across = jnp.where(low, zr[1].astype(F32), zr[2].astype(F32))
    square = square + fold(to_near * across) * (2.0 / 256.0)

    table = jnp.concatenate(moments + [square, jnp.zeros((64, LANES), F32)], 0)
    az[0] = jnp.sum(table.T, axis=0, keepdims=True)
    along_z = [copy(az.at[0], az.at[i], S_AZ, at(dz=i // 2, dc=i % 2)) for i in range(1, 2 * NZ)]
    all_z = copy(az.at[pl.ds(1, 2 * NZ - 1)], az.at[pl.ds(1, 2 * NZ - 1)], S_AZ, near[4])
    for i in sorted(range(1, 2 * NZ), key=lambda i: -min(i // 2, NZ - i // 2)):
        along_z[i - 1].start()
    pl.semaphore_wait(x1, 3)
    for device in (at(dx=-1), at(dx=1)):
        signal(x2, device)
    for j in range(STRIPS):
        for i in range(2):
            ps[j, i] = products[i][:, j * LANES : (j + 1) * LANES]
    fields[3].start()
    pl.semaphore_wait(x2, 2)
    signal(x3, at(dx=-1))
    shares = []
    for j, (dx, dc) in enumerate([(dx, dc) for dx in range(NX) for dc in range(2)][1:]):
        device = at(dx=dx, dc=dc)
        shares.append(copy(ps.at[device["probe"]], pr.at[j], S_P, device))
    for send in shares:
        send.start()
    all_shares = copy(pr, pr, S_P, near[4])

    for send in sends + fields + [to_partner, all_shares]:
        send.wait_send()
    pl.semaphore_wait(x3, 1)
    all_z.wait_recv()
    ay[0] = jnp.sum(az[...], axis=0)
    plane = [copy(ay.at[0], ay.at[i], S_AY, at(dx=i // NY, dy=i % NY)) for i in range(1, NX * NY)]
    for i in sorted(range(1, NX * NY), key=lambda i: -(min(i // NY, NX - i // NY) + min(i % NY, NY - i % NY))):
        plane[i - 1].start()
    all_plane = copy(ay.at[pl.ds(1, NX * NY - 1)], ay.at[pl.ds(1, NX * NY - 1)], S_AY, near[4])
    all_z.wait_send()
    fields[3].wait_recv()
    all_shares.wait_recv()
    all_plane.wait_recv()
    m0 = jnp.concatenate([jnp.sum(ay[NY * i : NY * (i + 1)], axis=0) for i in range(NX)], 0)
    m1, m2, m3 = (pltpu.roll(m0, LANES - CHIP * i, 1) for i in (1, 2, 3))
    step0 = m0 / m1
    growth = m2 / m1
    step1 = (m2 - m1 * m1 / m0) / (m3 - m2 * growth)
    alpha, beta = step0 + step0 * step1 * growth, -step0 * step1
    at_lane = lax.broadcasted_iota(jnp.int32, (1, LANES), 1)
    packed = jnp.zeros((1, LANES), F32)
    for i in range(NX):
        for h, value in enumerate((alpha, beta)):
            first = 32 * i + CHIP * h
            row = value[i : i + 1]
            if first:
                row = pltpu.roll(row, first, 1)
            packed = jnp.where((at_lane >= first) & (at_lane < first + CHIP), row, packed)
    coef[...] = jnp.broadcast_to(packed, (LANES, LANES)).T

    mine = pl.ds(pl.multiple_of(c * HALF, HALF), HALF)
    alpha_mine = jnp.concatenate([coef[mine, :]] * STRIPS, 1)
    beta_mine = jnp.concatenate([coef[pl.ds(pl.multiple_of(CHIP + c * HALF, HALF), HALF), :]] * STRIPS, 1)
    sol[c] = alpha_mine * pv[c] + beta_mine * zf[mine, :]
    sol[other] = alpha_mine * pv[other] + beta_mine * zx[...]
    for dc, tile in ((0, c), (1, other)):
        total = jnp.zeros((CHIP, LANES), F32)
        for dx in range(NX):
            share = ps.at[k] if (dx, dc) == (0, 0) else pr.at[2 * dx + dc - 1]
            total = total + coef[32 * dx : 32 * dx + CHIP, :] * share[0]
            total = total + coef[32 * dx + CHIP : 32 * dx + 2 * CHIP, :] * share[1]
        var[pl.ds(tile, 1), :] = jnp.sum(total, axis=0, keepdims=True) * (1.0 / PROBES)
    all_plane.wait_send()


def shards(coords, noise_var, probes, pair_list):
    anywhere = pl.BlockSpec(memory_space=pl.ANY)
    return pl.pallas_call(
        kernel,
        out_shape=(
            jax.ShapeDtypeStruct(probes.shape, F32),
            jax.ShapeDtypeStruct((2, LANES), F32),
        ),
        in_specs=[anywhere] * 4,
        out_specs=[pl.BlockSpec(memory_space=pltpu.VMEM)] * 2,
        scratch_shapes=[
            pltpu.SMEM((2, 4), jnp.int32),
            pltpu.VMEM((3, 2, 2, PTS), F32),
            pltpu.VMEM((4, 2, PTS), F32),
            pltpu.VMEM((2, PTS, LANES), F32),
            pltpu.VMEM((2, PTS), F32),
            pltpu.VMEM((2, HALF, PTS), F32),
            pltpu.VMEM((3, 2, 2 * HALF, PTS), BF16),
            pltpu.VMEM((2, HALF, PTS), F32),
            pltpu.VMEM((2, CHIP, PTS), BF16),
            pltpu.VMEM((PTS, PTS), BF16),
            pltpu.VMEM((PTS, PTS), BF16),
            pltpu.VMEM((PTS, 2 * PTS), BF16),
            pltpu.VMEM((CHIP, 2 * PTS), BF16),
            pltpu.VMEM((CHIP, PTS), F32),
            pltpu.VMEM((CHIP, PTS), F32),
            pltpu.VMEM((CHIP, PTS), F32),
            pltpu.VMEM((CHIP, PTS), BF16),
            pltpu.VMEM((3, CHIP, PTS), BF16),
            pltpu.VMEM((HALF, PTS), F32),
            pltpu.VMEM((2 * NZ, 1, LANES), F32),
            pltpu.VMEM((NX * NY, 1, LANES), F32),
            pltpu.VMEM((LANES, LANES), F32),
            pltpu.VMEM((8, 2, CHIP, LANES), F32),
            pltpu.VMEM((7, 2, CHIP, LANES), F32),
            pltpu.SemaphoreType.DMA((4,)),
            pltpu.SemaphoreType.DMA((N_SEMS,)),
            pltpu.SemaphoreType.DMA((N_SEMS,)),
            pltpu.SemaphoreType.REGULAR,
            pltpu.SemaphoreType.REGULAR,
            pltpu.SemaphoreType.REGULAR,
            pltpu.SemaphoreType.REGULAR,
            pltpu.SemaphoreType.REGULAR,
            pltpu.SemaphoreType.REGULAR,
        ],
        compiler_params=pltpu.CompilerParams(
            collective_id=0, has_side_effects=True, vmem_limit_bytes=32 << 20
        ),
    )(*(pltpu.with_memory_space_constraint(v, pltpu.MemorySpace.HBM) for v in (coords, noise_var, probes, pair_list)))


def solution(mesh):
    in_specs = (
        P("tiles", None, None),
        P("tiles", None),
        P("tiles", "probe", None),
        P("tiles", None),
    )
    out_specs = (P("tiles", "probe", None), P("tiles", "probe"))
    return jax.shard_map(shards, mesh=mesh, in_specs=in_specs, out_specs=out_specs, check_vma=False)
```
